32 devices in a mesh: seq: 8 (over z, x), ch: 4 (over y, core).
Axes of the slice: x: 2, y: 2, z: 4, core: 2. Of those that a mesh axis runs over, the one named last changes fastest.
Arguments:
- activations: bfloat16 [16384, 4096], P('seq', 'ch'), may hold values from -16 to 16
- gate_input: bfloat16 [16384, 4096], P('seq', 'ch'), may hold values from -6 to 6
- bmat: bfloat16 [16384, 128], P('seq'), may hold values from -0.29882812 to 0.29882812
- cmat: bfloat16 [16384, 128], P('seq'), may hold values from -0.29882812 to 0.29882812
- log_fwd: float32 [64, 16384], P('ch', 'seq'), may hold values from -0.6 to 0
- log_rev: float32 [64, 16384], P('ch', 'seq'), may hold values from -0.6 to 0
- skip: float32 [64], P('ch'), may hold values from 0.5 to 2
- gain: float32 [4096], P('ch'), may hold values from 0.1 to 1.9
Outputs:
- normed: bfloat16 [16384, 4096], P('seq', 'ch')
The draws below stay inside these ranges and needn't reach their ends.
All inputs are finite; a program needn't handle non-finite values.
Results may differ from the reference program's by a relative error of at most 0.0013.
Values sent between devices are 32-bit elements; how exact they have to be, the bound alone decides.
No kernel may reach another device: no remote copies, remote signals or barrier semaphores. Data moves between devices by JAX's collectives and lax.ppermute only.
A program may use at most 256 MiB of HBM per device.

```python
import math
import jax
import jax.numpy as jnp
from jax import lax

INNER = 4096
HEADDIM = 64
STATE = 128
BLOCK = 512
TOK_DEV = 2048
SCAN_HEADS = 64
WINDOW_TOKENS = 16384


def decay_law(key, fast_share):
    variety_key, quick_key, gradual_key, stretch_key, jagged_key, spike_key, depth_key = jax.random.split(key, 7)
    fast_head = jax.random.uniform(variety_key, (SCAN_HEADS, 1)) < fast_share
    fast_rate = jnp.exp(jax.random.uniform(quick_key, (SCAN_HEADS, 1), minval=math.log(1.0 / 50.0), maxval=math.log(1.0 / 30.0)))
    slow_rate = jnp.exp(jax.random.uniform(gradual_key, (SCAN_HEADS, 1), minval=math.log(0.1 / WINDOW_TOKENS), maxval=math.log(0.5 / WINDOW_TOKENS)))
    decay_speed = jnp.where(fast_head, fast_rate, slow_rate)
    stretch = jnp.exp(jax.random.uniform(stretch_key, (SCAN_HEADS, WINDOW_TOKENS // TOK_DEV), minval=math.log(0.5), maxval=0.0))
    stretch = jnp.repeat(stretch, TOK_DEV, axis=1)
    jaggedness = jax.random.uniform(jagged_key, (SCAN_HEADS, WINDOW_TOKENS), minval=0.5, maxval=1.5)
    locations = jax.random.randint(spike_key, (2,), 0, WINDOW_TOKENS)
    spiked_sites = jnp.any(jnp.arange(WINDOW_TOKENS)[None, :] == locations[:, None], axis=0)
    spike_depth = jax.random.uniform(depth_key, (SCAN_HEADS, WINDOW_TOKENS), minval=0.22, maxval=0.5)
    return -(decay_speed * stretch * jaggedness) - jnp.where(spiked_sites[None, :], spike_depth, 0.0)


def draw_log_fwd(key, part):
    key = jax.random.fold_in(key, 11)
    return decay_law(key, 0.5)


def draw_log_rev(key, part):
    key = jax.random.fold_in(key, 23)
    return decay_law(key, 0.5)


def draw_activations(key, part):
    key = jax.random.fold_in(key, 5)
    key_base, key_column, key_row = jax.random.split(key, 3)
    column_ramp = 3.0
    row_low = 0.5
    row_high = 2.0
    base = jax.random.normal(key_base, (WINDOW_TOKENS, INNER), jnp.float32)
    column = column_ramp ** (jnp.arange(INNER, dtype=jnp.float32) / INNER) * jax.random.uniform(key_column, (INNER,), minval=0.6, maxval=1.6)
    row = jnp.exp(jax.random.uniform(key_row, (WINDOW_TOKENS, 1), minval=math.log(row_low), maxval=math.log(row_high)))
    return jnp.clip(base * column[None, :] * row, -16.0, 16.0).astype(jnp.bfloat16)


def level_of(own_key, shape, cuts, least, largest):
    level, own = 1.0, jax.random.fold_in(own_key, 6)
    for dim, blocks in cuts:
        heights = jnp.exp(jax.random.uniform(jax.random.fold_in(own, dim), (blocks,), jnp.float32, least / len(cuts), largest / len(cuts)))
        level = level * jnp.repeat(heights, shape[dim] // blocks).reshape([-1 if axis == dim else 1 for axis in range(len(shape))])
    return level


def scatter_about(stream_key, extent, width, bound, cuts=(), kind=jnp.bfloat16):
    values = width * jax.random.normal(stream_key, extent, jnp.float32)
    if cuts:
        values = values * level_of(stream_key, extent, cuts, -0.22, 0.18)
    return jnp.clip(values, -bound, bound).astype(kind)


def setup_inputs(seed: int = 0) -> dict:
    seeds = jax.random.split(jax.random.key(seed), 9)
    return {
        "activations": draw_activations(jax.random.fold_in(seeds[8], 71), 0),
        "gate_input": scatter_about(seeds[1], (WINDOW_TOKENS, INNER), 1.0, 6.0, ((0, 8), (1, 4))),
        "bmat": scatter_about(seeds[2], (WINDOW_TOKENS, STATE), 0.042, 0.29882812, ((0, 8),)),
        "cmat": scatter_about(seeds[3], (WINDOW_TOKENS, STATE), 0.042, 0.29882812, ((0, 8),)),
        "log_fwd": draw_log_fwd(jax.random.fold_in(seeds[8], 71), 0),
        "log_rev": draw_log_rev(jax.random.fold_in(seeds[8], 71), 0),
        "skip": jnp.clip(0.5 + 1.5 * jax.random.uniform(seeds[6], (SCAN_HEADS,), jnp.float32) ** level_of(seeds[6], (SCAN_HEADS,), ((0, 4),), -0.2, 0.2), 0.5, 2.0),
        "gain": jnp.clip(1.0 + 0.18 * jax.random.normal(seeds[7], (INNER,), jnp.float32), 0.1, 1.9),
    }


def block_step(carry_state, x_block, b_block, c_block, log_block):
    exact = lax.Precision.HIGHEST
    cumulative = jnp.cumsum(log_block, axis=1)
    scores = jnp.dot(c_block, b_block.T, preferred_element_type=jnp.float32)
    spread = cumulative[:, :, None] - cumulative[:, None, :]
    length = log_block.shape[1]
    lower_mask = (jnp.arange(length)[:, None] >= jnp.arange(length)[None, :])[None]
    decay_matrix = jnp.where(lower_mask, jnp.exp(jnp.where(lower_mask, spread, 0.0)), 0.0)
    weights = lax.optimization_barrier((decay_matrix * scores[None]).astype(jnp.bfloat16))
    within = jnp.einsum('hij,jhp->ihp', weights.astype(jnp.float32), x_block.astype(jnp.float32), precision=exact)
    c_scaled = jnp.exp(cumulative)[:, :, None] * c_block.astype(jnp.float32)[None]
    carried = jnp.einsum('hin,hpn->ihp', c_scaled, carry_state, precision=exact)
    to_end = jnp.exp(cumulative[:, -1:] - cumulative)
    b_scaled = lax.optimization_barrier((to_end[:, :, None] * b_block.astype(jnp.float32)[None]).astype(jnp.bfloat16))
    fresh_term = jnp.einsum('jhp,hjn->hpn', x_block.astype(jnp.float32), b_scaled.astype(jnp.float32), precision=exact)
    next_state = jnp.exp(cumulative[:, -1])[:, None, None] * carry_state + fresh_term
    return (within + carried, next_state)

def scan_direction(x_heads, b_rows, c_rows, log_rows):
    total = x_heads.shape[0]
    blocks = total // BLOCK
    heads = x_heads.shape[1]
    headdim = x_heads.shape[2]
    x_blocks = x_heads.reshape(blocks, BLOCK, heads, headdim)
    b_blocks = b_rows.reshape(blocks, BLOCK, b_rows.shape[1])
    c_blocks = c_rows.reshape(blocks, BLOCK, c_rows.shape[1])
    log_blocks = log_rows.reshape(heads, blocks, BLOCK).transpose(1, 0, 2)

    def advance(carry_state, block):
        out_block, next_state = block_step(carry_state, block[0], block[1], block[2], block[3])
        return (next_state, out_block)
    start_state = jnp.zeros((heads, headdim, b_rows.shape[1]), jnp.float32)
    final_state, outputs = lax.scan(advance, start_state, (x_blocks, b_blocks, c_blocks, log_blocks))
    return outputs.reshape(total, heads, headdim)

def reference(activations, gate_input, bmat, cmat, log_fwd, log_rev, skip, gain):
    x_heads = activations.reshape(WINDOW_TOKENS, SCAN_HEADS, HEADDIM)
    forward = scan_direction(x_heads, bmat, cmat, log_fwd)
    backward = scan_direction(x_heads[::-1], bmat[::-1], cmat[::-1], log_rev[:, ::-1])[::-1]
    combined = forward + backward + skip[None, :, None] * x_heads.astype(jnp.float32)
    combined = combined.reshape(WINDOW_TOKENS, INNER)
    gated = combined * jax.nn.silu(gate_input.astype(jnp.float32))
    mean_square = lax.optimization_barrier(jnp.mean(gated * gated, axis=1, keepdims=True))
    return (gated * lax.rsqrt(mean_square + 1e-05) * gain[None, :]).astype(jnp.bfloat16)
```

```python
import functools

import jax
import jax.numpy as jnp
from jax import lax
from jax.experimental import pallas as pl
from jax.experimental.pallas import tpu as pltpu
from jax.sharding import PartitionSpec as P

INNER = 4096
BLOCK = 512
TILE = 128
LOG2E = 1.4426950408889634
VMEM = 56 * 1024 * 1024
F32, BF16 = jnp.float32, jnp.bfloat16


def running_sum(log, reverse):
    length = log.shape[1]
    lane = lax.broadcasted_iota(jnp.int32, log.shape, 1)
    total, shift = log, 1
    while shift < length:
        if reverse:
            moved, inside = pltpu.roll(total, length - shift, 1), lane < length - shift
        else:
            moved, inside = pltpu.roll(total, shift, 1), lane >= shift
        total = total + jnp.where(inside, moved, 0.0)
        shift *= 2
    return total


def spread_heads(column, headdim):
    heads = column.shape[0]
    head = lax.broadcasted_iota(jnp.int32, (heads, heads * headdim), 0)
    lane = lax.broadcasted_iota(jnp.int32, (heads, heads * headdim), 1)
    return jnp.sum(jnp.where(lane // headdim == head, column, 0.0), axis=0, keepdims=True)


def states_kernel(headdim, x_ref, b_ref, lf_ref, lr_ref, cum_ref, fresh_ref, drow_ref, final_ref):
    k = pl.program_id(0)
    heads = lf_ref.shape[0]
    state = b_ref.shape[1]

    @pl.when(k == 0)
    def _():
        final_ref[:, :state] = jnp.zeros((2, state, final_ref.shape[2]), F32)
        final_ref[:, state:] = jnp.ones((2, 8, final_ref.shape[2]), F32)

    cf = running_sum(lf_ref[...], False) * LOG2E
    cr = running_sum(lr_ref[...], True) * LOG2E
    lf, lr = cf[:, BLOCK - 1 :], cr[:, :1]
    ef, er = jnp.exp2(lf - cf), jnp.exp2(lr - cr)
    df, dr = spread_heads(jnp.exp2(lf), headdim), spread_heads(jnp.exp2(lr), headdim)
    drow_ref[0] = jnp.concatenate([df, dr, jnp.zeros((6, df.shape[1]), F32)], axis=0)
    b_t = b_ref[...].astype(F32).T
    lane = lax.broadcasted_iota(jnp.int32, (state, 2 * headdim), 1)
    for p in range(heads // 2):
        h = 2 * p
        cum_ref[p] = jnp.concatenate(
            [cf[h : h + 2], cr[h : h + 2], jnp.zeros((4, BLOCK), F32)], axis=0
        )
        rows = jnp.concatenate(
            [(b_t * e[g : g + 1]).astype(BF16) for g in (h, h + 1) for e in (ef, er)], axis=0
        )
        cols = slice(2 * headdim * p, 2 * headdim * (p + 1))
        both = jnp.dot(rows, x_ref[:, cols], preferred_element_type=F32)
        fresh_f = jnp.where(lane < headdim, both[:state], both[2 * state : 3 * state])
        fresh_r = jnp.where(lane < headdim, both[state : 2 * state], both[3 * state :])
        fresh_ref[0, 0, :, cols] = fresh_f
        fresh_ref[1, 0, :, cols] = fresh_r
        final_ref[0, :state, cols] = final_ref[0, :state, cols] * df[:, cols] + fresh_f
        final_ref[1, :state, cols] += final_ref[1, state : state + 1, cols] * fresh_r
    final_ref[0, state:] = final_ref[0, state:] * df
    final_ref[1, state:] = final_ref[1, state:] * dr


def within_kernel(headdim, x_ref, b_ref, c_ref, cum_ref, skip_ref, out_ref, score_ref):
    tiles = BLOCK // TILE
    scores = lax.dot_general(
        c_ref[...], b_ref[...], (((1,), (1,)), ((), ())), preferred_element_type=F32
    )
    row = lax.broadcasted_iota(jnp.int32, (BLOCK, BLOCK), 0)
    col = lax.broadcasted_iota(jnp.int32, (BLOCK, BLOCK), 1)
    score_ref[...] = jnp.where(row == col, 2.0 * scores, scores)
    lane = lax.broadcasted_iota(jnp.int32, (BLOCK, 2 * headdim), 1)
    lower = lax.broadcasted_iota(jnp.int32, (TILE, TILE), 0) >= lax.broadcasted_iota(
        jnp.int32, (TILE, TILE), 1
    )

    @pl.loop(0, cum_ref.shape[0])
    def _(p):
        cum = cum_ref[p]
        cum_t = cum.T
        cols = pl.ds(pl.multiple_of(p * 2 * headdim, 2 * headdim), 2 * headdim)
        x = x_ref[:, cols]
        parts = []
        for q in range(2):
            lines = []
            for i in range(tiles):
                at = slice(i * TILE, (i + 1) * TILE)
                cf, cr = cum_t[at, q : q + 1], cum_t[at, 2 + q : 3 + q]
                pieces = []
                for j in range(tiles):
                    to = slice(j * TILE, (j + 1) * TILE)
                    rf, rr = cum[q : q + 1, to], cum[2 + q : 3 + q, to]
                    if j < i:
                        gap = cf - rf
                    elif j > i:
                        gap = cr - rr
                    else:
                        gap = jnp.where(lower, cf - rf, cr - rr)
                    pieces.append((jnp.exp2(gap) * score_ref[at, to]).astype(BF16))
                lines.append(jnp.concatenate(pieces, axis=1))
            weights = jnp.concatenate(lines, axis=0)
            parts.append(jnp.dot(weights, x, preferred_element_type=F32))
        y = jnp.where(lane < headdim, parts[0], parts[1])
        out_ref[:, cols] = y + skip_ref[:, cols] * x.astype(F32)


def halves(value):
    high = value.astype(BF16)
    return jnp.concatenate([high, (value - high.astype(F32)).astype(BF16)], axis=0)


def carried_kernel(
    headdim, a_ref, gate_ref, c_ref, cum_ref, drow_ref, fresh_ref, in_ref, out_ref, sq_ref, st_ref, hot_ref
):
    k = pl.program_id(0)
    blocks = fresh_ref.shape[1]
    pairs = cum_ref.shape[0]
    channels = a_ref.shape[1]

    @pl.when(k == 0)
    def _():
        row = lax.broadcasted_iota(jnp.int32, (16 * pairs, channels), 0)
        head = lax.broadcasted_iota(jnp.int32, (16 * pairs, channels), 1) // headdim
        row = lax.rem(row, 8 * pairs)
        for d in range(2):
            mine = row == 8 * (head // 2) + lax.rem(head, 2) + 2 * d
            hot_ref[d] = jnp.where(mine, 1.0, 0.0).astype(BF16)
        for d in range(2):
            total = in_ref[d]
            for step in range(blocks):
                at = step if d == 0 else blocks - 1 - step
                st_ref[d, at] = halves(total)
                if step < blocks - 1:
                    total = total * drow_ref[at, d : d + 1] + fresh_ref[d, at]

    decay = jnp.exp2(cum_ref[...].reshape(8 * pairs, BLOCK))
    high = decay.astype(BF16).astype(F32)
    decay_t = jnp.concatenate([high, decay - high], axis=0).T.astype(BF16)
    c = c_ref[...]
    cc = jnp.concatenate([c, c], axis=1)
    wide = 256
    squares = jnp.zeros((BLOCK, 128), F32)
    for n in range(channels // wide):
        cols = slice(n * wide, (n + 1) * wide)
        total = a_ref[:, cols]
        for d in range(2):
            scale = jnp.dot(decay_t, hot_ref[d, :, cols], preferred_element_type=F32)
            total = total + scale * jnp.dot(cc, st_ref[d, k, :, cols], preferred_element_type=F32)
        gate = gate_ref[:, cols].astype(F32)
        gated = total * (gate / (1.0 + jnp.exp(-gate)))
        out_ref[:, cols] = gated
        square = gated * gated
        for m in range(wide // 128):
            squares = squares + square[:, m * 128 : (m + 1) * 128]
    sq_ref[0] = jnp.sum(squares.T, axis=0, keepdims=True)


def norm_kernel(gated_ref, sq_ref, gain_ref, out_ref):
    factor = lax.rsqrt(sq_ref[0] * (1.0 / INNER) + 1e-05)
    factor = jnp.broadcast_to(factor, (128, factor.shape[1])).T
    for n in range(gated_ref.shape[1] // 128):
        cols = slice(n * 128, (n + 1) * 128)
        out_ref[:, cols] = (gated_ref[:, cols] * factor * gain_ref[:, cols]).astype(BF16)


def params():
    return pltpu.CompilerParams(vmem_limit_bytes=VMEM, dimension_semantics=("arbitrary",))


def across(value, pairs):
    return lax.ppermute(value, "seq", pairs)


def incoming(final):
    count, mine = lax.axis_size("seq"), lax.axis_index("seq")
    rows, row, side = count // 2, mine // 2, mine % 2
    state, half = final.shape[1] - 8, final.shape[2] // 2
    first, second = final[:, :, :half], final[:, :, half:]
    swap = [(i, i ^ 1) for i in range(count)]
    kept = jnp.where(side == 0, first, second)
    got = across(jnp.where(side == 0, second, first), swap)
    low, high = jnp.where(side == 0, kept, got), jnp.where(side == 0, got, kept)
    low_d, high_d = low[:, state : state + 1], high[:, state : state + 1]
    low, high = low[:, :state], high[:, :state]
    pair_f, pair_r = high_d[0] * low[0] + high[0], low_d[1] * high[1] + low[1]
    pair_d = low_d * high_d
    enter_f = jnp.zeros_like(pair_f)
    enter_r = jnp.zeros_like(pair_r)
    for hop in range(rows - 1):
        back = rows - 1 - hop
        send = jnp.where(row == hop, pair_d[0] * enter_f + pair_f, pair_d[1] * enter_r + pair_r)
        route = [(2 * hop + s, 2 * hop + 2 + s) for s in range(2)]
        route += [(2 * back + s, 2 * back - 2 + s) for s in range(2)]
        got = across(send, route)
        enter_f = jnp.where(row == hop + 1, got, enter_f)
        enter_r = jnp.where(row == back - 1, got, enter_r)
    at_low = jnp.stack([enter_f, high_d[1] * enter_r + high[1]])
    at_high = jnp.stack([low_d[0] * enter_f + low[0], enter_r])
    got = across(jnp.where(side == 0, at_high, at_low), swap)
    kept = jnp.where(side == 0, at_low, at_high)
    return jnp.concatenate(
        [jnp.where(side == 0, kept, got), jnp.where(side == 0, got, kept)], axis=2
    )


def shards(activations, gate_input, bmat, cmat, log_fwd, log_rev, skip, gain):
    length, channels = activations.shape
    heads = log_fwd.shape[0]
    headdim = channels // heads
    pairs = heads // 2
    state = bmat.shape[1]
    blocks = length // BLOCK
    tall = pl.BlockSpec((BLOCK, channels), lambda k: (k, 0))
    thin = pl.BlockSpec((BLOCK, state), lambda k: (k, 0))
    logs = pl.BlockSpec((heads, BLOCK), lambda k: (0, k))
    cums = pl.BlockSpec((pairs, 8, BLOCK), lambda k: (0, 0, k))
    line = pl.BlockSpec((1, channels), lambda k: (0, 0))
    tiny = pl.BlockSpec((1, 1, BLOCK), lambda k: (k, 0, 0))
    cum, fresh, drow, final = pl.pallas_call(
        functools.partial(states_kernel, headdim),
        grid=(blocks,),
        in_specs=[tall, thin, logs, logs],
        out_specs=[
            cums,
            pl.BlockSpec((2, 1, state, channels), lambda k: (0, k, 0, 0)),
            pl.BlockSpec((1, 8, channels), lambda k: (k, 0, 0)),
            pl.BlockSpec((2, state + 8, channels), lambda k: (0, 0, 0)),
        ],
        out_shape=[
            jax.ShapeDtypeStruct((pairs, 8, length), F32),
            jax.ShapeDtypeStruct((2, blocks, state, channels), F32),
            jax.ShapeDtypeStruct((blocks, 8, channels), F32),
            jax.ShapeDtypeStruct((2, state + 8, channels), F32),
        ],
        compiler_params=params(),
        name="states",
    )(activations, bmat, log_fwd, log_rev)
    skip_row = jnp.repeat(skip, headdim)[None]
    within = pl.pallas_call(
        functools.partial(within_kernel, headdim),
        grid=(blocks,),
        in_specs=[tall, thin, thin, cums, line],
        out_specs=tall,
        out_shape=jax.ShapeDtypeStruct((length, channels), F32),
        scratch_shapes=[pltpu.VMEM((BLOCK, BLOCK), F32)],
        compiler_params=params(),
        cost_estimate=pl.CostEstimate(
            flops=2 * heads * length * BLOCK * 128, bytes_accessed=6 * length * channels,
            transcendentals=heads * length * BLOCK,
        ),
        name="within",
    )(activations, bmat, cmat, cum, skip_row)
    enter = incoming(final)
    gated, squares = pl.pallas_call(
        functools.partial(carried_kernel, headdim),
        grid=(blocks,),
        in_specs=[
            tall,
            tall,
            thin,
            cums,
            pl.BlockSpec((blocks, 8, channels), lambda k: (0, 0, 0)),
            pl.BlockSpec((2, blocks, state, channels), lambda k: (0, 0, 0, 0)),
            pl.BlockSpec((2, state, channels), lambda k: (0, 0, 0)),
        ],
        out_specs=[tall, tiny],
        out_shape=[
            jax.ShapeDtypeStruct((length, channels), F32),
            jax.ShapeDtypeStruct((blocks, 1, BLOCK), F32),
        ],
        scratch_shapes=[
            pltpu.VMEM((2, blocks, 2 * state, channels), BF16),
            pltpu.VMEM((2, 16 * pairs, channels), BF16),
        ],
        compiler_params=params(),
        name="carried",
    )(within, gate_input, cmat, cum, drow, fresh, enter)
    step, size = 1, lax.axis_size("ch")
    while step < size:
        squares = squares + lax.ppermute(squares, "ch", [(i, i ^ step) for i in range(size)])
        step *= 2
    return pl.pallas_call(
        norm_kernel,
        grid=(blocks,),
        in_specs=[tall, tiny, line],
        out_specs=tall,
        out_shape=jax.ShapeDtypeStruct((length, channels), BF16),
        compiler_params=params(),
        name="norm",
    )(gated, squares, gain[None])


def solution(mesh):
    return jax.shard_map(
        shards,
        mesh=mesh,
        in_specs=(
            P("seq", "ch"),
            P("seq", "ch"),
            P("seq", None),
            P("seq", None),
            P("ch", "seq"),
            P("ch", "seq"),
            P("ch"),
            P("ch"),
        ),
        out_specs=P("seq", "ch"),
        check_vma=False,
    )
```

```python
import functools

import jax
import jax.numpy as jnp
from jax import lax
from jax.experimental import pallas as pl
from jax.experimental.pallas import tpu as pltpu
from jax.sharding import PartitionSpec as P

INNER = 4096
BLOCK = 512
TILE = 128
TILES = BLOCK // TILE
GROUPS = 1
LOG2E = 1.4426950408889634
F32, BF16 = jnp.float32, jnp.bfloat16
ANY = pl.BlockSpec(memory_space=pl.ANY)


def shape(*dims, dtype=F32):
    return jax.ShapeDtypeStruct(dims, dtype)


def far(*values):
    return [pltpu.with_memory_space_constraint(value, pltpu.HBM) for value in values]


def near(*values):
    return [pltpu.with_memory_space_constraint(value, pltpu.VMEM) for value in values]


def params(mib):
    return pltpu.CompilerParams(
        vmem_limit_bytes=mib * 1024 * 1024, dimension_semantics=("arbitrary",)
    )


def running_sums(log, reverse):
    heads, length = log.shape
    rows = jnp.concatenate(
        [log[:, at : at + BLOCK] for at in range(0, length, BLOCK)], axis=0
    )
    high = rows.astype(BF16)
    rest = rows - high.astype(F32)
    middle = rest.astype(BF16)
    low = (rest - middle.astype(F32)).astype(BF16)
    u = lax.broadcasted_iota(jnp.int32, (BLOCK, BLOCK), 0)
    t = lax.broadcasted_iota(jnp.int32, (BLOCK, BLOCK), 1)
    taken = jnp.where(u >= t if reverse else u <= t, 1.0, 0.0).astype(BF16)
    total = [jnp.dot(part, taken, preferred_element_type=F32) for part in (low, middle, high)]
    return total[0] + total[1] + total[2]


def halves(value):
    high = value.astype(BF16)
    return jnp.concatenate([high, (value - high.astype(F32)).astype(BF16)], axis=0)


def states_kernel(headdim, chained, x_ref, b_ref, lf_ref, lr_ref, *refs):
    cum_ref, dev_ref, st_ref, final_ref, bt_ref, sum_ref = refs[3 if chained else 0 :]
    p = pl.program_id(0)
    pairs, blocks = sum_ref.shape[:2]
    state = b_ref.shape[1]

    @pl.when(p == 0)
    def _():
        cf = running_sums(lf_ref[...], False) * LOG2E
        cr = running_sums(lr_ref[...], True) * LOG2E
        for k in range(blocks):
            bt_ref[k] = b_ref[k * BLOCK : (k + 1) * BLOCK].astype(F32).T
            for i in range(pairs):
                h = slice(2 * (k * pairs + i), 2 * (k * pairs + i) + 2)
                sum_ref[i, k, 0:2] = cf[h]
                sum_ref[i, k, 2:4] = cr[h]
                sum_ref[i, k, 4:8] = jnp.zeros((4, BLOCK), F32)

    first = lax.broadcasted_iota(jnp.int32, (1, 2 * headdim), 1) < headdim
    lane = lax.broadcasted_iota(jnp.int32, (state, 2 * headdim), 1)
    forward = lax.broadcasted_iota(jnp.int32, (8, 1), 0) < 2
    fresh, decay, total = [], [], []
    for k in range(blocks):
        at = slice(k * BLOCK, (k + 1) * BLOCK)
        cum = sum_ref[p, k]
        last = jnp.where(forward, cum[:, BLOCK - 1 :], cum[:, :1])
        to_end = jnp.exp2(last - cum)
        whole = jnp.exp2(last)
        rows = jnp.concatenate(
            [(bt_ref[k] * to_end[r : r + 1]).astype(BF16) for r in range(4)], axis=0
        )
        both = jnp.dot(rows, x_ref[at], preferred_element_type=F32)
        fresh.append(
            [
                jnp.where(
                    lane < headdim,
                    both[2 * d * state : (2 * d + 1) * state],
                    both[(2 * d + 1) * state : (2 * d + 2) * state],
                )
                for d in range(2)
            ]
        )
        decay.append(
            [
                jnp.where(first, whole[2 * d : 2 * d + 1], whole[2 * d + 1 : 2 * d + 2])
                for d in range(2)
            ]
        )
        total.append(last)
        cum_ref[0, :, at] = cum
    for d in range(2):
        order = range(blocks) if d == 0 else range(blocks - 1, -1, -1)
        held = jnp.zeros_like(fresh[0][0])
        through = jnp.ones_like(decay[0][0])
        for k in order:
            st_ref[d, k] = halves(held)
            held = held * decay[k][d] + fresh[k][d]
            through = through * decay[k][d]
        final_ref[d, :state] = held
        final_ref[d, state:] = jnp.broadcast_to(through, (8, 2 * headdim))
    before = jnp.zeros((8, 1), F32)
    after = jnp.zeros((8, 1), F32)
    for k in range(blocks):
        at = slice(k * BLOCK, (k + 1) * BLOCK)
        back = slice((blocks - 1 - k) * BLOCK, (blocks - k) * BLOCK)
        dev_ref[0, 0:2, at] = (sum_ref[p, k] + before)[0:2]
        dev_ref[0, 2:4, back] = (sum_ref[p, blocks - 1 - k] + after)[2:4]
        dev_ref[0, 4:8, at] = jnp.zeros((4, BLOCK), F32)
        before = before + total[k]
        after = after + total[blocks - 1 - k]


def within_kernel(headdim, chained, x_ref, b_ref, c_ref, cum_ref, st_ref, skip_ref, dep_ref, *refs):
    out_ref, zero_ref, score_ref, row_ref, col_ref = refs[1 if chained else 0 :]
    width = 2 * headdim
    pairs = cum_ref.shape[0]
    zero_ref[...] = jnp.zeros_like(zero_ref)

    @pl.when(pl.program_id(0) == 0)
    def _():
        scores = lax.dot_general(
            c_ref[...], b_ref[...], (((1,), (1,)), ((), ())), preferred_element_type=F32
        )
        row = lax.broadcasted_iota(jnp.int32, (BLOCK, BLOCK), 0)
        col = lax.broadcasted_iota(jnp.int32, (BLOCK, BLOCK), 1)
        score_ref[...] = jnp.where(row == col, 2.0 * scores, scores)

    first = lax.broadcasted_iota(jnp.int32, (1, width), 1) < headdim
    lower = lax.broadcasted_iota(jnp.int32, (TILE, TILE), 0) >= lax.broadcasted_iota(
        jnp.int32, (TILE, TILE), 1
    )
    forward = lax.broadcasted_iota(jnp.int32, (8, 1), 0) < 2
    none = jnp.zeros((8, 1), F32)
    c = c_ref[...]
    cc = jnp.concatenate([c, c], axis=1)
    for p in range(pairs):
        cum = cum_ref[p]
        starts = []
        for i in range(TILES):
            lo = cum[:, i * TILE - 1 : i * TILE] if i else none
            hi = cum[:, (i + 1) * TILE : (i + 1) * TILE + 1] if i < TILES - 1 else none
            base = jnp.where(forward, lo, hi)
            row_ref[p, i] = jnp.exp2(base - cum)
            at = slice(i * TILE, (i + 1) * TILE)
            col_ref[p, :, at] = jnp.exp2(cum[:, at] - base)
            starts.append(jnp.exp2(base))
        cols = slice(p * width, (p + 1) * width)
        x = x_ref[:, cols]
        tall = []
        for i in range(TILES):
            at = slice(i * TILE, (i + 1) * TILE)
            tall.append(
                [jnp.broadcast_to(col_ref[p, r : r + 1, at], (TILE, TILE)).T for r in range(4)]
            )
        parts = []
        for q in range(2):
            lines = []
            for i in range(TILES):
                at = slice(i * TILE, (i + 1) * TILE)
                cf, cr = tall[i][q], tall[i][2 + q]
                pieces = []
                for j in range(TILES):
                    to = slice(j * TILE, (j + 1) * TILE)
                    rf = row_ref[p, i, q : q + 1, to]
                    rr = row_ref[p, i, 2 + q : 3 + q, to]
                    score = score_ref[at, to]
                    if j < i:
                        weight = (score * rf) * cf
                    elif j > i:
                        weight = (score * rr) * cr
                    else:
                        weight = score * jnp.where(lower, rf * cf, rr * cr)
                    pieces.append(weight.astype(BF16))
                lines.append(jnp.concatenate(pieces, axis=1))
            weights = jnp.concatenate(lines, axis=0)
            parts.append(jnp.dot(weights, x, preferred_element_type=F32))
        held = jnp.concatenate([st_ref[0, 0, :, cols], st_ref[1, 0, :, cols]], axis=1)
        z = jnp.dot(cc, held, preferred_element_type=F32)
        for i in range(TILES):
            at = slice(i * TILE, (i + 1) * TILE)
            y = jnp.where(first, parts[0][at], parts[1][at])
            y = y + skip_ref[:, cols] * x[at].astype(F32)
            for d in range(2):
                scale = jnp.where(first, starts[i][2 * d : 2 * d + 1], starts[i][2 * d + 1 : 2 * d + 2])
                scale = scale * jnp.where(first, tall[i][2 * d], tall[i][2 * d + 1])
                y = y + scale * z[at, d * width : (d + 1) * width]
            out_ref[at, cols] = y


def carried_kernel(headdim, chained, a_ref, gate_ref, c_ref, dev_ref, in_ref, *refs):
    out_ref, sq_ref, st_ref, hot_ref = refs[1 if chained else 0 :]
    pairs = dev_ref.shape[0]
    width = 2 * headdim

    @pl.when(pl.program_id(0) == 0)
    def _():
        row = lax.rem(lax.broadcasted_iota(jnp.int32, (16 * pairs, 2 * width), 0), 8 * pairs)
        lane = lax.broadcasted_iota(jnp.int32, (16 * pairs, 2 * width), 1)
        for p in range(pairs):
            hot = jnp.where(row == 8 * p + lane // headdim, 1.0, 0.0)
            hot_ref[:, 2 * width * p : 2 * width * (p + 1)] = hot.astype(BF16)
            for d in range(2):
                at = 2 * width * p + width * d
                st_ref[:, at : at + width] = halves(in_ref[d, :, p * width : (p + 1) * width])

    decay = jnp.exp2(dev_ref[...].reshape(8 * pairs, BLOCK))
    high = decay.astype(BF16).astype(F32)
    decay_t = jnp.concatenate([high, decay - high], axis=0).T.astype(BF16)
    c = c_ref[...]
    cc = jnp.concatenate([c, c], axis=1)
    squares = jnp.zeros((BLOCK, width), F32)
    for p in range(pairs):
        cols = slice(p * width, (p + 1) * width)
        wide = slice(2 * p * width, 2 * (p + 1) * width)
        scale = jnp.dot(decay_t, hot_ref[:, wide], preferred_element_type=F32)
        both = scale * jnp.dot(cc, st_ref[:, wide], preferred_element_type=F32)
        total = a_ref[:, cols] + both[:, :width] + both[:, width:]
        gate = gate_ref[:, cols].astype(F32)
        gated = total * (gate / (1.0 + jnp.exp(-gate)))
        out_ref[:, cols] = gated
        squares = squares + gated * gated
    sq_ref[0] = jnp.sum(squares.T, axis=0, keepdims=True)


def norm_kernel(gated_ref, sq_ref, gain_ref, out_ref):
    factor = lax.rsqrt(sq_ref[0] * (1.0 / INNER) + 1e-05)
    factor = jnp.broadcast_to(factor, (128, factor.shape[1])).T
    for n in range(gated_ref.shape[1] // 128):
        cols = slice(n * 128, (n + 1) * 128)
        out_ref[:, cols] = (gated_ref[:, cols] * factor * gain_ref[:, cols]).astype(BF16)


def incoming(finals, beside):
    count, mine = lax.axis_size("seq"), lax.axis_index("seq")
    rows, row, side = count // 2, mine // 2, mine % 2
    left, early = side == 0, row < rows // 2
    swap = [(i, i ^ 1) for i in range(count)]
    send = lambda value, route: lax.ppermute(value, "seq", route)
    groups = range(len(finals))
    stages = [[] for _ in groups]
    state, half = finals[0].shape[1] - 8, finals[0].shape[2] // 2
    kept, given, got1, got2 = {}, {}, {}, {}
    for g in groups:
        first, second = finals[g][:, :, :half], finals[g][:, :, half:]
        kept[g] = jnp.where(left, first, second)
        other = jnp.where(left, second, first)
        given[g] = jnp.where(early, other[0], other[1]), jnp.where(early, other[1], other[0])
        stages[g].append(given[g][0])
        got1[g] = send(given[g][0], swap)
    enter = {g: [jnp.zeros((state, half), F32)] * 2 for g in groups}
    low, high, dl, dh = {}, {}, {}, {}
    got, out1, out2 = {}, {}, {}

    def parts(g, d, arrived):
        mine_d = kept[g][d]
        lo, hi = jnp.where(left, mine_d, arrived), jnp.where(left, arrived, mine_d)
        return lo[:state], hi[:state], lo[state : state + 1], hi[state : state + 1]

    def pair(g, d, pieces):
        lo, hi, decay_lo, decay_hi = pieces
        if d == 0:
            return decay_hi * lo + hi, decay_lo * decay_hi
        return decay_lo * hi + lo, decay_lo * decay_hi

    def both(d, pieces, held):
        lo, hi, decay_lo, decay_hi = pieces
        if d == 0:
            return held, decay_lo * held + lo
        return decay_hi * held + hi, held

    def pick(flag, a, b):
        return jax.tree.map(lambda u, v: jnp.where(flag, u, v), a, b)

    token = early_token = beside(stages[0][-1])
    known = {}
    for hop in range(rows - 1):
        back = rows - 1 - hop
        route = [(2 * hop + s, 2 * hop + 2 + s) for s in range(2)]
        route += [(2 * back + s, 2 * back - 2 + s) for s in range(2)]
        for g in groups:
            if hop == 0:
                known[g] = [parts(g, d, got1[g]) for d in range(2)]
            if hop == rows // 2:
                second = [parts(g, d, got2[g] + token) for d in range(2)]
                known[g] = [pick(early, known[g][0], second[0]), pick(early, second[1], known[g][1])]
            (pf, df), (pr, dr) = pair(g, 0, known[g][0]), pair(g, 1, known[g][1])
            payload = jnp.where(row == hop, df * enter[g][0] + pf, dr * enter[g][1] + pr)
            payload = payload + token[:state]
            stages[g].append(payload)
            got[g] = send(payload, route)
        token = beside(stages[0][-1])
        for g in groups:
            if hop == 0:
                later = given[g][1] + (0.0 * got1[g] + early_token)
                got2[g] = send(later, swap)
            enter[g] = [
                jnp.where(row == hop + 1, got[g], enter[g][0]),
                jnp.where(row == back - 1, got[g], enter[g][1]),
            ]
            if hop == max(rows // 2 - 2, 0):
                ends = pick(early, both(0, known[g][0], enter[g][0]), both(1, known[g][1], enter[g][1]))
                out1[g] = (jnp.where(left, ends[0], ends[1]), send(jnp.where(left, ends[1], ends[0]), swap))
    result = []
    for g in groups:
        ends = pick(early, both(1, known[g][1], enter[g][1]), both(0, known[g][0], enter[g][0]))
        payload = jnp.where(left, ends[1], ends[0]) + token[:state]
        stages[g].append(payload)
        out2[g] = (jnp.where(left, ends[0], ends[1]), send(payload, swap))
        whole = []
        for own, came in (out1[g], out2[g]):
            whole.append(
                jnp.concatenate([jnp.where(left, own, came), jnp.where(left, came, own)], axis=1)
            )
        result.append(
            jnp.stack([jnp.where(early, whole[0], whole[1]), jnp.where(early, whole[1], whole[0])])
        )
    return result


def shards(activations, gate_input, bmat, cmat, log_fwd, log_rev, skip, gain):
    length, channels = activations.shape
    heads = log_fwd.shape[0]
    headdim = channels // heads
    width = 2 * headdim
    state = bmat.shape[1]
    blocks = length // BLOCK
    pairs = heads // 2
    mine = pairs // GROUPS
    part = channels // GROUPS
    finals = []
    shared = []
    for g in range(GROUPS):
        done = list(shared)
        *shared, final = pl.pallas_call(
            functools.partial(states_kernel, headdim, bool(done)),
            grid=(mine,),
            in_specs=[
                pl.BlockSpec((length, width), lambda p, g=g: (0, g * mine + p)),
                pl.BlockSpec((length, state), lambda p: (0, 0)),
                pl.BlockSpec((2 * mine, length), lambda p, g=g: (g, 0)),
                pl.BlockSpec((2 * mine, length), lambda p, g=g: (g, 0)),
            ]
            + [ANY] * len(done),
            out_specs=[
                pl.BlockSpec((1, 8, length), lambda p, g=g: (g * mine + p, 0, 0)),
                pl.BlockSpec((1, 8, length), lambda p, g=g: (g * mine + p, 0, 0)),
                pl.BlockSpec((2, blocks, 2 * state, width), lambda p, g=g: (0, 0, 0, g * mine + p)),
                pl.BlockSpec((2, state + 8, width), lambda p: (0, 0, p)),
            ],
            out_shape=[
                pltpu.HBM((pairs, 8, length), F32),
                pltpu.HBM((pairs, 8, length), F32),
                pltpu.HBM((2, blocks, 2 * state, channels), BF16),
                shape(2, state + 8, part),
            ],
            scratch_shapes=[
                pltpu.VMEM((blocks, state, BLOCK), F32),
                pltpu.VMEM((mine, blocks, 8, BLOCK), F32),
            ],
            input_output_aliases={4 + i: i for i in range(len(done))},
            compiler_params=params(16),
            name="states",
        )(*far(activations, bmat, log_fwd, log_rev, *done))
        finals.append(final)
    cum, dev, held = shared
    skip_row = jnp.repeat(skip, headdim)[None]
    within = []
    some = 2
    left = list(range(blocks))

    def piece(dep):
        if not left:
            return jnp.zeros((state + 8, part // 2), F32)
        k = left.pop(0)
        done = list(within)
        within[:], zero = (lambda out: ([out[0]], [out[1]]))(
            pl.pallas_call(
                functools.partial(within_kernel, headdim, bool(done)),
                grid=(pairs // some,),
                in_specs=[
                    pl.BlockSpec((BLOCK, some * width), lambda n: (k, n)),
                    pl.BlockSpec((BLOCK, state), lambda n: (k, 0)),
                    pl.BlockSpec((BLOCK, state), lambda n: (k, 0)),
                    pl.BlockSpec((some, 8, BLOCK), lambda n: (n, 0, k)),
                    pl.BlockSpec((2, 1, 2 * state, some * width), lambda n: (0, k, 0, n)),
                    pl.BlockSpec((1, some * width), lambda n: (0, n)),
                    ANY,
                ]
                + [ANY] * len(done),
                out_specs=[
                    pl.BlockSpec((BLOCK, some * width), lambda n: (k, n)),
                    pl.BlockSpec((state + 8, part // 2), lambda n: (0, 0)),
                ],
                out_shape=[pltpu.HBM((length, channels), F32), shape(state + 8, part // 2)],
                scratch_shapes=[
                    pltpu.VMEM((BLOCK, BLOCK), F32),
                    pltpu.VMEM((some, TILES, 8, BLOCK), F32),
                    pltpu.VMEM((some, 8, BLOCK), F32),
                ],
                input_output_aliases={7: 0} if done else {},
                compiler_params=params(16),
                cost_estimate=pl.CostEstimate(
                    flops=2 * heads * BLOCK * BLOCK * 512,
                    bytes_accessed=6 * BLOCK * channels,
                    transcendentals=heads * BLOCK * 8,
                ),
                name="within",
            )(*far(activations, bmat, cmat, cum, held), skip_row, dep, *far(*done))
        )
        return zero[0]

    enters = incoming(finals, piece)
    while left:
        piece(finals[0])
    gated = []
    squares = 0.0
    for g in range(GROUPS):
        tall = pl.BlockSpec((BLOCK, part), lambda k, g=g: (k, g))
        gated, square = pl.pallas_call(
            functools.partial(carried_kernel, headdim, bool(gated)),
            grid=(blocks,),
            in_specs=[
                tall,
                tall,
                pl.BlockSpec((BLOCK, state), lambda k: (k, 0)),
                pl.BlockSpec((mine, 8, BLOCK), lambda k, g=g: (g, 0, k)),
                pl.BlockSpec((2, state, part), lambda k: (0, 0, 0)),
            ]
            + [ANY] * len(gated),
            out_specs=[tall, pl.BlockSpec((1, 1, BLOCK), lambda k: (k, 0, 0))],
            out_shape=[pltpu.VMEM((length, channels), F32), shape(blocks, 1, BLOCK)],
            scratch_shapes=[
                pltpu.VMEM((2 * state, 2 * part), BF16),
                pltpu.VMEM((16 * mine, 2 * part), BF16),
            ],
            input_output_aliases={5: 0} if gated else {},
            compiler_params=params(24),
            name="carried",
        )(*far(within[0], gate_input, cmat, dev), enters[g], *near(*gated))
        gated = [gated]
        squares = squares + square
    step, size = 1, lax.axis_size("ch")
    while step < size:
        squares = squares + lax.ppermute(squares, "ch", [(i, i ^ step) for i in range(size)])
        step *= 2
    tall = pl.BlockSpec((BLOCK, channels), lambda k: (k, 0))
    return pl.pallas_call(
        norm_kernel,
        grid=(blocks,),
        in_specs=[
            tall,
            pl.BlockSpec((1, 1, BLOCK), lambda k: (k, 0, 0)),
            pl.BlockSpec((1, channels), lambda k: (0, 0)),
        ],
        out_specs=tall,
        out_shape=shape(length, channels, dtype=BF16),
        compiler_params=params(16),
        name="norm",
    )(*near(gated[0]), squares, gain[None])


def solution(mesh):
    return jax.shard_map(
        shards,
        mesh=mesh,
        in_specs=(
            P("seq", "ch"),
            P("seq", "ch"),
            P("seq", None),
            P("seq", None),
            P("ch", "seq"),
            P("ch", "seq"),
            P("ch"),
            P("ch"),
        ),
        out_specs=P("seq", "ch"),
        check_vma=False,
    )
```

```python
import functools

import jax
import jax.numpy as jnp
from jax import lax
from jax.experimental import pallas as pl
from jax.experimental.pallas import tpu as pltpu
from jax.sharding import PartitionSpec as P

INNER = 4096
BLOCK = 512
TILE = 128
TILES = BLOCK // TILE
GROUPS = 1
PIECES = 5
LOG2E = 1.4426950408889634
F32, BF16 = jnp.float32, jnp.bfloat16
ANY = pl.BlockSpec(memory_space=pl.ANY)


def shape(*dims, dtype=F32):
    return jax.ShapeDtypeStruct(dims, dtype)


def far(*values):
    return [pltpu.with_memory_space_constraint(value, pltpu.HBM) for value in values]


def near(*values):
    return [pltpu.with_memory_space_constraint(value, pltpu.VMEM) for value in values]


def params(mib):
    return pltpu.CompilerParams(
        vmem_limit_bytes=mib * 1024 * 1024, dimension_semantics=("arbitrary",)
    )


def running_sums(log, reverse):
    heads, length = log.shape
    rows = jnp.concatenate(
        [log[:, at : at + BLOCK] for at in range(0, length, BLOCK)], axis=0
    )
    high = rows.astype(BF16)
    rest = rows - high.astype(F32)
    middle = rest.astype(BF16)
    low = (rest - middle.astype(F32)).astype(BF16)
    u = lax.broadcasted_iota(jnp.int32, (BLOCK, BLOCK), 0)
    t = lax.broadcasted_iota(jnp.int32, (BLOCK, BLOCK), 1)
    taken = jnp.where(u >= t if reverse else u <= t, 1.0, 0.0).astype(BF16)
    total = [jnp.dot(part, taken, preferred_element_type=F32) for part in (low, middle, high)]
    return total[0] + total[1] + total[2]


def halves(value):
    high = value.astype(BF16)
    return jnp.concatenate([high, (value - high.astype(F32)).astype(BF16)], axis=0)


def states_kernel(headdim, chained, x_ref, b_ref, lf_ref, lr_ref, *refs):
    cum_ref, before_ref, off_ref, final_ref, bt_ref, sum_ref = refs[3 if chained else 0 :]
    step = pl.program_id(0)
    pairs, blocks = sum_ref.shape[:2]
    state = b_ref.shape[1]

    @pl.when(step == 0)
    def _():
        cf = running_sums(lf_ref[...], False) * LOG2E
        cr = running_sums(lr_ref[...], True) * LOG2E
        for k in range(blocks):
            bt_ref[k] = b_ref[k * BLOCK : (k + 1) * BLOCK].astype(F32).T
            for i in range(pairs):
                h = slice(2 * (k * pairs + i), 2 * (k * pairs + i) + 2)
                sum_ref[i, k, 0:2] = cf[h]
                sum_ref[i, k, 2:4] = cr[h]
                sum_ref[i, k, 4:8] = jnp.zeros((4, BLOCK), F32)

    first = lax.broadcasted_iota(jnp.int32, (1, 2 * headdim), 1) < headdim
    lane = lax.broadcasted_iota(jnp.int32, (state, 2 * headdim), 1)
    forward = lax.broadcasted_iota(jnp.int32, (8, 1), 0) < 2
    for one in range(cum_ref.shape[0]):
        p = step * cum_ref.shape[0] + one
        cols = slice(2 * headdim * one, 2 * headdim * (one + 1))
        fresh, decay = [], []
        for k in range(blocks):
            at = slice(k * BLOCK, (k + 1) * BLOCK)
            cum = sum_ref[p, k]
            last = jnp.where(forward, cum[:, BLOCK - 1 :], cum[:, :1])
            to_end = jnp.exp2(last - cum)
            whole = jnp.exp2(last)
            rows = jnp.concatenate(
                [(bt_ref[k] * to_end[r : r + 1]).astype(BF16) for r in range(4)], axis=0
            )
            both = jnp.dot(rows, x_ref[at, cols], preferred_element_type=F32)
            fresh.append(
                [
                    jnp.where(
                        lane < headdim,
                        both[2 * d * state : (2 * d + 1) * state],
                        both[(2 * d + 1) * state : (2 * d + 2) * state],
                    )
                    for d in range(2)
                ]
            )
            decay.append(
                [
                    jnp.where(first, whole[2 * d : 2 * d + 1], whole[2 * d + 1 : 2 * d + 2])
                    for d in range(2)
                ]
            )
            cum_ref[one, :, at] = cum
        for d in range(2):
            order = range(blocks) if d == 0 else range(blocks - 1, -1, -1)
            held = jnp.zeros_like(fresh[0][0])
            through = jnp.ones_like(decay[0][0])
            for k in order:
                before_ref[k, d, :, cols] = held
                off_ref[k, d : d + 1, cols] = through
                held = held * decay[k][d] + fresh[k][d]
                through = through * decay[k][d]
            final_ref[d, :state, cols] = held
            final_ref[d, state:, cols] = jnp.broadcast_to(through, (8, 2 * headdim))


def within_kernel(headdim, chunks, first_unit, chained, x_ref, b_ref, c_ref, cum_ref, skip_ref, dep_ref, *refs):
    out_ref, zero_ref, score_ref, row_ref, col_ref = refs[1 if chained else 0 :]
    width = 2 * headdim
    pairs = cum_ref.shape[0]
    zero_ref[...] = jnp.zeros_like(zero_ref)

    unit = first_unit + pl.program_id(0)

    @pl.when((pl.program_id(0) == 0) | (lax.rem(unit, chunks) == 0))
    def _():
        scores = lax.dot_general(
            c_ref[...], b_ref[...], (((1,), (1,)), ((), ())), preferred_element_type=F32
        )
        row = lax.broadcasted_iota(jnp.int32, (BLOCK, BLOCK), 0)
        col = lax.broadcasted_iota(jnp.int32, (BLOCK, BLOCK), 1)
        score_ref[...] = jnp.where(row == col, 2.0 * scores, scores)

    first = lax.broadcasted_iota(jnp.int32, (1, width), 1) < headdim
    lower = lax.broadcasted_iota(jnp.int32, (TILE, TILE), 0) >= lax.broadcasted_iota(
        jnp.int32, (TILE, TILE), 1
    )
    forward = lax.broadcasted_iota(jnp.int32, (8, 1), 0) < 2
    none = jnp.zeros((8, 1), F32)
    for p in range(pairs):
        cum = cum_ref[p]
        for i in range(TILES):
            lo = cum[:, i * TILE - 1 : i * TILE] if i else none
            hi = cum[:, (i + 1) * TILE : (i + 1) * TILE + 1] if i < TILES - 1 else none
            base = jnp.where(forward, lo, hi)
            row_ref[p, i] = jnp.exp2(base - cum)
            at = slice(i * TILE, (i + 1) * TILE)
            col_ref[p, :, at] = jnp.exp2(cum[:, at] - base)
        cols = slice(p * width, (p + 1) * width)
        x = x_ref[:, cols]
        parts = []
        for q in range(2):
            done = []
            for i in range(TILES):
                at = slice(i * TILE, (i + 1) * TILE)
                cf, cr = [
                    jnp.broadcast_to(col_ref[p, r : r + 1, at], (TILE, TILE)).T for r in (q, 2 + q)
                ]
                pieces = []
                for j in range(TILES):
                    to = slice(j * TILE, (j + 1) * TILE)
                    rf = row_ref[p, i, q : q + 1, to]
                    rr = row_ref[p, i, 2 + q : 3 + q, to]
                    score = score_ref[at, to]
                    if j < i:
                        weight = (score * rf) * cf
                    elif j > i:
                        weight = (score * rr) * cr
                    else:
                        weight = score * jnp.where(lower, rf * cf, rr * cr)
                    pieces.append(weight.astype(BF16))
                line = jnp.concatenate(pieces, axis=1)
                if i % 2:
                    both = jnp.concatenate([line_before, line], axis=0)
                    done.append(jnp.dot(both, x, preferred_element_type=F32))
                line_before = line
            parts.append(jnp.concatenate(done, axis=0))
        y = jnp.where(first, parts[0], parts[1])
        out_ref[:, cols] = y + skip_ref[:, cols] * x.astype(F32)


def carried_kernel(headdim, chained, a_ref, gate_ref, c_ref, cum_ref, before_ref, off_ref, in_ref, *refs):
    out_ref, sq_ref, hot_ref = refs[1 if chained else 0 :]
    pairs = cum_ref.shape[0]
    width = 2 * headdim

    @pl.when(pl.program_id(0) == 0)
    def _():
        row = lax.broadcasted_iota(jnp.int32, (16 * pairs, 1), 0)
        row = jnp.where(row < 8 * pairs, row, row - 8 * pairs)
        lane = lax.broadcasted_iota(jnp.int32, (1, width), 1)
        for p in range(pairs):
            hot = jnp.where(row == 8 * p + 2 + jnp.where(lane < headdim, 0, 1), 1.0, 0.0)
            hot_ref[:, p * width : (p + 1) * width] = hot.astype(BF16)

    every = jnp.exp2(cum_ref[...].reshape(8 * pairs, BLOCK))
    high = every.astype(BF16).astype(F32)
    every_t = jnp.concatenate([high, every - high], axis=0).T.astype(BF16)
    c = c_ref[...]
    cc = jnp.concatenate([c, c], axis=1)
    squares = [jnp.zeros((TILE, width), F32)] * TILES
    for p in range(pairs):
        cols = slice(p * width, (p + 1) * width)
        decay = every[8 * p : 8 * p + 8]
        if p % 2 == 0:
            scales = jnp.dot(every_t, hot_ref[:, p * width : (p + 2) * width], preferred_element_type=F32)
        held = [
            halves(before_ref[0, d, :, cols] + off_ref[0, d : d + 1, cols] * in_ref[d, :, cols])
            for d in range(2)
        ]
        z = jnp.dot(cc, jnp.concatenate(held, axis=1), preferred_element_type=F32)
        for i in range(TILES):
            at = slice(i * TILE, (i + 1) * TILE)
            rows = [jnp.broadcast_to(decay[r : r + 1, at], (headdim, TILE)) for r in range(2)]
            total = a_ref[at, cols] + jnp.concatenate(rows, axis=0).T * z[at, :width]
            total = total + scales[at, p % 2 * width : (p % 2 + 1) * width] * z[at, width:]
            half = 0.5 * gate_ref[at, cols].astype(F32)
            gated = total * (half + half * jnp.tanh(half))
            out_ref[at, cols] = gated
            squares[i] = squares[i] + gated * gated
    for i in range(TILES):
        sq_ref[0, :, i * TILE : (i + 1) * TILE] = jnp.sum(squares[i].T, axis=0, keepdims=True)


def norm_kernel(gated_ref, sq_ref, gain_ref, out_ref):
    factor = lax.rsqrt(sq_ref[0] * (1.0 / INNER) + 1e-05)
    factor = jnp.broadcast_to(factor, (128, factor.shape[1])).T
    for n in range(gated_ref.shape[1] // 128):
        cols = slice(n * 128, (n + 1) * 128)
        out_ref[:, cols] = (gated_ref[:, cols] * factor * gain_ref[:, cols]).astype(BF16)


def incoming(finals, beside):
    count, mine = lax.axis_size("seq"), lax.axis_index("seq")
    rows, row, side = count // 2, mine // 2, mine % 2
    left, early = side == 0, row < rows // 2
    swap = [(i, i ^ 1) for i in range(count)]
    send = lambda value, route: lax.ppermute(value, "seq", route)
    groups = range(len(finals))
    stages = [[] for _ in groups]
    state, half = finals[0].shape[1] - 8, finals[0].shape[2] // 2
    kept, given, got1, got2 = {}, {}, {}, {}
    for g in groups:
        first, second = finals[g][:, :, :half], finals[g][:, :, half:]
        kept[g] = jnp.where(left, first, second)
        other = jnp.where(left, second, first)
        given[g] = jnp.where(early, other[0], other[1]), jnp.where(early, other[1], other[0])
        stages[g].append(given[g][0])
        got1[g] = send(given[g][0], swap)
    enter = {g: [jnp.zeros((state, half), F32)] * 2 for g in groups}
    low, high, dl, dh = {}, {}, {}, {}
    got, out1, out2 = {}, {}, {}

    def parts(g, d, arrived):
        mine_d = kept[g][d]
        lo, hi = jnp.where(left, mine_d, arrived), jnp.where(left, arrived, mine_d)
        return lo[:state], hi[:state], lo[state : state + 1], hi[state : state + 1]

    def pair(g, d, pieces):
        lo, hi, decay_lo, decay_hi = pieces
        if d == 0:
            return decay_hi * lo + hi, decay_lo * decay_hi
        return decay_lo * hi + lo, decay_lo * decay_hi

    def both(d, pieces, held):
        lo, hi, decay_lo, decay_hi = pieces
        if d == 0:
            return held, decay_lo * held + lo
        return decay_hi * held + hi, held

    def pick(flag, a, b):
        return jax.tree.map(lambda u, v: jnp.where(flag, u, v), a, b)

    token = early_token = beside(stages[0][-1])
    known = {}
    for hop in range(rows - 1):
        back = rows - 1 - hop
        route = [(2 * hop + s, 2 * hop + 2 + s) for s in range(2)]
        route += [(2 * back + s, 2 * back - 2 + s) for s in range(2)]
        for g in groups:
            if hop == 0:
                known[g] = [parts(g, d, got1[g]) for d in range(2)]
            if hop == rows // 2:
                second = [parts(g, d, got2[g] + token) for d in range(2)]
                known[g] = [pick(early, known[g][0], second[0]), pick(early, second[1], known[g][1])]
            (pf, df), (pr, dr) = pair(g, 0, known[g][0]), pair(g, 1, known[g][1])
            payload = jnp.where(row == hop, df * enter[g][0] + pf, dr * enter[g][1] + pr)
            payload = payload + token
            stages[g].append(payload)
            got[g] = send(payload, route)
        token = beside(stages[0][-1])
        for g in groups:
            if hop == 0:
                later = given[g][1] + (0.0 * got1[g] + early_token)
                got2[g] = send(later, swap)
            enter[g] = [
                jnp.where(row == hop + 1, got[g], enter[g][0]),
                jnp.where(row == back - 1, got[g], enter[g][1]),
            ]
            if hop == max(rows // 2 - 2, 0):
                ends = pick(early, both(0, known[g][0], enter[g][0]), both(1, known[g][1], enter[g][1]))
                out1[g] = (jnp.where(left, ends[0], ends[1]), send(jnp.where(left, ends[1], ends[0]), swap))
    result = []
    for g in groups:
        ends = pick(early, both(1, known[g][1], enter[g][1]), both(0, known[g][0], enter[g][0]))
        payload = jnp.where(left, ends[1], ends[0]) + token
        stages[g].append(payload)
        out2[g] = (jnp.where(left, ends[0], ends[1]), send(payload, swap))
    beside(stages[0][-1])
    for g in groups:
        whole = []
        for own, came in (out1[g], out2[g]):
            whole.append(
                jnp.concatenate([jnp.where(left, own, came), jnp.where(left, came, own)], axis=1)
            )
        result.append(
            jnp.stack([jnp.where(early, whole[0], whole[1]), jnp.where(early, whole[1], whole[0])])
        )
    return result


def shards(activations, gate_input, bmat, cmat, log_fwd, log_rev, skip, gain):
    length, channels = activations.shape
    heads = log_fwd.shape[0]
    headdim = channels // heads
    width = 2 * headdim
    state = bmat.shape[1]
    blocks = length // BLOCK
    pairs = heads // 2
    mine = pairs // GROUPS
    part = channels // GROUPS
    many = 2
    finals = []
    shared = []
    for g in range(GROUPS):
        done = list(shared)
        *shared, final = pl.pallas_call(
            functools.partial(states_kernel, headdim, bool(done)),
            grid=(mine // many,),
            in_specs=[
                pl.BlockSpec((length, many * width), lambda n, g=g: (0, g * mine // many + n)),
                pl.BlockSpec((length, state), lambda n: (0, 0)),
                pl.BlockSpec((2 * mine, length), lambda n, g=g: (g, 0)),
                pl.BlockSpec((2 * mine, length), lambda n, g=g: (g, 0)),
            ]
            + [ANY] * len(done),
            out_specs=[
                pl.BlockSpec((many, 8, length), lambda n, g=g: (g * mine // many + n, 0, 0)),
                pl.BlockSpec(
                    (blocks, 2, state, many * width),
                    lambda n, g=g: (0, 0, 0, g * mine // many + n),
                ),
                pl.BlockSpec((blocks, 8, many * width), lambda n, g=g: (0, 0, g * mine // many + n)),
                pl.BlockSpec((2, state + 8, many * width), lambda n: (0, 0, n)),
            ],
            out_shape=[
                pltpu.HBM((pairs, 8, length), F32),
                pltpu.HBM((blocks, 2, state, channels), F32),
                pltpu.HBM((blocks, 8, channels), F32),
                shape(2, state + 8, part),
            ],
            scratch_shapes=[
                pltpu.VMEM((blocks, state, BLOCK), F32),
                pltpu.VMEM((mine, blocks, 8, BLOCK), F32),
            ],
            input_output_aliases={4 + i: i for i in range(len(done))},
            compiler_params=params(24),
            name="states",
        )(*far(activations, bmat, log_fwd, log_rev, *done))
        finals.append(final)
    cum, before, off = shared
    skip_row = jnp.repeat(skip, headdim)[None]
    within = []
    some = 2
    chunks = pairs // some
    units = blocks * chunks
    cuts = [units * i // PIECES for i in range(PIECES + 1)]
    plan = list(zip(cuts[:-1], cuts[1:]))[::-1]

    def piece(dep):
        if not plan:
            return jnp.zeros((1, part // 2), F32)
        start, stop = plan.pop()
        block, chunk = lambda n: (start + n) // chunks, lambda n: lax.rem(start + n, chunks)
        done = list(within)
        within[:1], zero = (lambda out: ([out[0]], out[1]))(
            pl.pallas_call(
                functools.partial(within_kernel, headdim, chunks, start, bool(done)),
                grid=(stop - start,),
                in_specs=[
                    pl.BlockSpec((BLOCK, some * width), lambda n: (block(n), chunk(n))),
                    pl.BlockSpec((BLOCK, state), lambda n: (block(n), 0)),
                    pl.BlockSpec((BLOCK, state), lambda n: (block(n), 0)),
                    pl.BlockSpec((some, 8, BLOCK), lambda n: (chunk(n), 0, block(n))),
                    pl.BlockSpec((1, some * width), lambda n: (0, chunk(n))),
                    ANY,
                ]
                + [ANY] * len(done),
                out_specs=[
                    pl.BlockSpec((BLOCK, some * width), lambda n: (block(n), chunk(n))),
                    pl.BlockSpec((8, part // 2), lambda n: (0, 0)),
                ],
                out_shape=[pltpu.HBM((length, channels), F32), shape(8, part // 2)],
                scratch_shapes=[
                    pltpu.VMEM((BLOCK, BLOCK), F32),
                    pltpu.VMEM((some, TILES, 8, BLOCK), F32),
                    pltpu.VMEM((some, 8, BLOCK), F32),
                ],
                input_output_aliases={6: 0} if done else {},
                compiler_params=params(16),
                cost_estimate=pl.CostEstimate(
                    flops=2 * heads * BLOCK * BLOCK * 512,
                    bytes_accessed=6 * BLOCK * channels,
                    transcendentals=heads * BLOCK * 8,
                ),
                name="within",
            )(*far(activations, bmat, cmat, cum), skip_row, dep, *far(*done))
        )
        return zero[:1]

    enters = incoming(finals, piece)
    while plan:
        piece(finals[0])
    gated = []
    squares = 0.0
    for g in range(GROUPS):
        tall = pl.BlockSpec((BLOCK, part), lambda k, g=g: (k, g))
        gated, square = pl.pallas_call(
            functools.partial(carried_kernel, headdim, bool(gated)),
            grid=(blocks,),
            in_specs=[
                tall,
                tall,
                pl.BlockSpec((BLOCK, state), lambda k: (k, 0)),
                pl.BlockSpec((mine, 8, BLOCK), lambda k, g=g: (g, 0, k)),
                pl.BlockSpec((1, 2, state, part), lambda k, g=g: (k, 0, 0, g)),
                pl.BlockSpec((1, 8, part), lambda k, g=g: (k, 0, g)),
                pl.BlockSpec((2, state, part), lambda k: (0, 0, 0)),
            ]
            + [ANY] * len(gated),
            out_specs=[tall, pl.BlockSpec((1, 1, BLOCK), lambda k: (k, 0, 0))],
            out_shape=[pltpu.VMEM((length, channels), F32), shape(blocks, 1, BLOCK)],
            scratch_shapes=[
                pltpu.VMEM((16 * mine, part), BF16),
            ],
            input_output_aliases={7: 0} if gated else {},
            compiler_params=params(24),
            name="carried",
        )(*far(within[0], gate_input, cmat, cum, before, off), enters[g], *near(*gated))
        gated = [gated]
        squares = squares + square
    step, size = 1, lax.axis_size("ch")
    while step < size:
        squares = squares + lax.ppermute(squares, "ch", [(i, i ^ step) for i in range(size)])
        step *= 2
    tall = pl.BlockSpec((BLOCK, channels), lambda k: (k, 0))
    return pl.pallas_call(
        norm_kernel,
        grid=(blocks,),
        in_specs=[
            tall,
            pl.BlockSpec((1, 1, BLOCK), lambda k: (k, 0, 0)),
            pl.BlockSpec((1, channels), lambda k: (0, 0)),
        ],
        out_specs=tall,
        out_shape=shape(length, channels, dtype=BF16),
        compiler_params=params(16),
        name="norm",
    )(*near(gated[0]), squares, gain[None])


def solution(mesh):
    return jax.shard_map(
        shards,
        mesh=mesh,
        in_specs=(
            P("seq", "ch"),
            P("seq", "ch"),
            P("seq", None),
            P("seq", None),
            P("ch", "seq"),
            P("ch", "seq"),
            P("ch"),
            P("ch"),
        ),
        out_specs=P("seq", "ch"),
        check_vma=False,
    )
```

```python
import functools

import jax
import jax.numpy as jnp
from jax import lax
from jax.experimental import pallas as pl
from jax.experimental.pallas import tpu as pltpu
from jax.sharding import PartitionSpec as P

INNER = 4096
BLOCK = 512
TILE = 128
TILES = BLOCK // TILE
GROUPS = 1
SHARES = (4, 8, 11, 13, 16)
LOG2E = 1.4426950408889634
F32, BF16 = jnp.float32, jnp.bfloat16
ANY = pl.BlockSpec(memory_space=pl.ANY)
WHOLE = pl.BlockSpec(memory_space=pltpu.VMEM)


def shape(*dims, dtype=F32):
    return jax.ShapeDtypeStruct(dims, dtype)


def far(*values):
    return [pltpu.with_memory_space_constraint(value, pltpu.HBM) for value in values]


def near(*values):
    return [pltpu.with_memory_space_constraint(value, pltpu.VMEM) for value in values]


def params(mib):
    return pltpu.CompilerParams(
        vmem_limit_bytes=mib * 1024 * 1024, dimension_semantics=("arbitrary",)
    )


def running_sums(log, reverse):
    heads, length = log.shape
    rows = jnp.concatenate(
        [log[:, at : at + BLOCK] for at in range(0, length, BLOCK)], axis=0
    )
    high = rows.astype(BF16)
    rest = rows - high.astype(F32)
    middle = rest.astype(BF16)
    low = (rest - middle.astype(F32)).astype(BF16)
    u = lax.broadcasted_iota(jnp.int32, (BLOCK, BLOCK), 0)
    t = lax.broadcasted_iota(jnp.int32, (BLOCK, BLOCK), 1)
    taken = jnp.where(u >= t if reverse else u <= t, 1.0, 0.0).astype(BF16)
    total = [jnp.dot(part, taken, preferred_element_type=F32) for part in (low, middle, high)]
    return total[0] + total[1] + total[2]


def halves(value):
    high = value.astype(BF16)
    return jnp.concatenate([high, (value - high.astype(F32)).astype(BF16)], axis=0)


def states_kernel(headdim, chained, x_ref, b_ref, lf_ref, lr_ref, *refs):
    cum_ref, before_ref, off_ref, final_ref, bt_ref, sum_ref = refs[3 if chained else 0 :]
    step = pl.program_id(0)
    pairs, blocks = sum_ref.shape[:2]
    state = b_ref.shape[1]

    @pl.when(step == 0)
    def _():
        cf = running_sums(lf_ref[...], False) * LOG2E
        cr = running_sums(lr_ref[...], True) * LOG2E
        for k in range(blocks):
            bt_ref[k] = b_ref[k * BLOCK : (k + 1) * BLOCK].astype(F32).T
            for i in range(pairs):
                h = slice(2 * (k * pairs + i), 2 * (k * pairs + i) + 2)
                sum_ref[i, k, 0:2] = cf[h]
                sum_ref[i, k, 2:4] = cr[h]
                sum_ref[i, k, 4:8] = jnp.zeros((4, BLOCK), F32)

    first = lax.broadcasted_iota(jnp.int32, (1, 2 * headdim), 1) < headdim
    lane = lax.broadcasted_iota(jnp.int32, (state, 2 * headdim), 1)
    forward = lax.broadcasted_iota(jnp.int32, (8, 1), 0) < 2
    for one in range(cum_ref.shape[0]):
        p = step * cum_ref.shape[0] + one
        cols = slice(2 * headdim * one, 2 * headdim * (one + 1))
        fresh, decay = [], []
        for k in range(blocks):
            at = slice(k * BLOCK, (k + 1) * BLOCK)
            cum = sum_ref[p, k]
            last = jnp.where(forward, cum[:, BLOCK - 1 :], cum[:, :1])
            to_end = jnp.exp2(last - cum)
            whole = jnp.exp2(last)
            x = x_ref[at, cols]
            both = []
            for q in range(2):
                rows = [(bt_ref[k] * to_end[r : r + 1]).astype(BF16) for r in (q, 2 + q)]
                both.append(
                    jnp.dot(jnp.concatenate(rows, axis=0), x, preferred_element_type=F32)
                )
            fresh.append(
                [
                    jnp.where(
                        lane < headdim,
                        both[0][d * state : (d + 1) * state],
                        both[1][d * state : (d + 1) * state],
                    )
                    for d in range(2)
                ]
            )
            decay.append(
                [
                    jnp.where(first, whole[2 * d : 2 * d + 1], whole[2 * d + 1 : 2 * d + 2])
                    for d in range(2)
                ]
            )
            cum_ref[one, :, at] = cum
        for d in range(2):
            order = range(blocks) if d == 0 else range(blocks - 1, -1, -1)
            held = jnp.zeros_like(fresh[0][0])
            through = jnp.ones_like(decay[0][0])
            for k in order:
                before_ref[k, d, :, cols] = held
                off_ref[k, d : d + 1, cols] = through
                held = held * decay[k][d] + fresh[k][d]
                through = through * decay[k][d]
            final_ref[d, :state, cols] = held
            final_ref[d, state:, cols] = jnp.broadcast_to(through, (8, 2 * headdim))


def within_kernel(headdim, chunks, first_unit, chained, x_ref, b_ref, c_ref, cum_ref, skip_ref, dep_ref, *refs):
    out_ref, zero_ref, score_ref, row_ref, col_ref = refs[1 if chained else 0 :]
    width = 2 * headdim
    pairs = cum_ref.shape[0]
    zero_ref[...] = jnp.zeros_like(zero_ref)

    unit = first_unit + pl.program_id(0)

    @pl.when((pl.program_id(0) == 0) | (lax.rem(unit, chunks) == 0))
    def _():
        scores = lax.dot_general(
            c_ref[...], b_ref[...], (((1,), (1,)), ((), ())), preferred_element_type=F32
        )
        row = lax.broadcasted_iota(jnp.int32, (BLOCK, BLOCK), 0)
        col = lax.broadcasted_iota(jnp.int32, (BLOCK, BLOCK), 1)
        score_ref[...] = jnp.where(row == col, 2.0 * scores, scores)

    first = lax.broadcasted_iota(jnp.int32, (1, width), 1) < headdim
    lower = lax.broadcasted_iota(jnp.int32, (TILE, TILE), 0) >= lax.broadcasted_iota(
        jnp.int32, (TILE, TILE), 1
    )
    forward = lax.broadcasted_iota(jnp.int32, (8, 1), 0) < 2
    none = jnp.zeros((8, 1), F32)
    for p in range(pairs):
        cum = cum_ref[p]
        for i in range(TILES):
            lo = cum[:, i * TILE - 1 : i * TILE] if i else none
            hi = cum[:, (i + 1) * TILE : (i + 1) * TILE + 1] if i < TILES - 1 else none
            base = jnp.where(forward, lo, hi)
            row_ref[p, i] = jnp.exp2(base - cum)
            at = slice(i * TILE, (i + 1) * TILE)
            col_ref[p, :, at] = jnp.exp2(cum[:, at] - base)
        cols = slice(p * width, (p + 1) * width)
        x = x_ref[:, cols]
        parts = []
        for q in range(2):
            done = []
            for i in range(TILES):
                at = slice(i * TILE, (i + 1) * TILE)
                cf, cr = [
                    jnp.broadcast_to(col_ref[p, r : r + 1, at], (TILE, TILE)).T for r in (q, 2 + q)
                ]
                pieces = []
                for j in range(TILES):
                    to = slice(j * TILE, (j + 1) * TILE)
                    rf = row_ref[p, i, q : q + 1, to]
                    rr = row_ref[p, i, 2 + q : 3 + q, to]
                    score = score_ref[at, to]
                    if j < i:
                        weight = (score * rf) * cf
                    elif j > i:
                        weight = (score * rr) * cr
                    else:
                        weight = score * jnp.where(lower, rf * cf, rr * cr)
                    pieces.append(weight.astype(BF16))
                line = jnp.concatenate(pieces, axis=1)
                if i % 2:
                    both = jnp.concatenate([line_before, line], axis=0)
                    done.append(jnp.dot(both, x, preferred_element_type=F32))
                line_before = line
            parts.append(jnp.concatenate(done, axis=0))
        y = jnp.where(first, parts[0], parts[1])
        out_ref[:, cols] = y + skip_ref[:, cols] * x.astype(F32)


def fetch(source, target, sem):
    copy = pltpu.make_async_copy(source, target, sem)
    copy.start()
    return copy


def carried_kernel(headdim, a_hbm, gate_hbm, c_hbm, cum_hbm, before_hbm, off_hbm, in_ref, out_ref, sq_ref, *refs):
    a_buf, gate_buf, c_buf, cum_buf, before_buf, off_buf, hot_ref, sems = refs
    blocks, pairs = a_buf.shape[0], cum_buf.shape[1]
    width = 2 * headdim

    def copies(k):
        at = pl.ds(pl.multiple_of(k * BLOCK, BLOCK), BLOCK)
        pieces = [
            (before_hbm.at[k], before_buf.at[k]),
            (off_hbm.at[k], off_buf.at[k]),
            (c_hbm.at[at], c_buf.at[k]),
            (cum_hbm.at[:, :, at], cum_buf.at[k]),
            (gate_hbm.at[at], gate_buf.at[k]),
            (a_hbm.at[at], a_buf.at[k]),
        ]
        return [pltpu.make_async_copy(f, t, sems.at[n, k]) for n, (f, t) in enumerate(pieces)]

    for k in range(blocks):
        for copy in copies(k):
            copy.start()
    row = lax.broadcasted_iota(jnp.int32, (16 * pairs, 1), 0)
    row = jnp.where(row < 8 * pairs, row, row - 8 * pairs)
    lane = lax.broadcasted_iota(jnp.int32, (1, width), 1)
    for p in range(pairs):
        hot = jnp.where(row == 8 * p + 2 + jnp.where(lane < headdim, 0, 1), 1.0, 0.0)
        hot_ref[:, p * width : (p + 1) * width] = hot.astype(BF16)

    @pl.loop(0, blocks)
    def _(k):
        for copy in copies(k):
            copy.wait()
        every = jnp.exp2(cum_buf[k].reshape(8 * pairs, BLOCK))
        high = every.astype(BF16).astype(F32)
        every_t = jnp.concatenate([high, every - high], axis=0).T.astype(BF16)
        c = c_buf[k]
        cc = jnp.concatenate([c, c], axis=1)
        squares = [jnp.zeros((TILE, width), F32)] * TILES
        scales = [None, None]
        for p in range(pairs):
            cols = slice(p * width, (p + 1) * width)
            decay = every[8 * p : 8 * p + 8]
            held = [
                halves(before_buf[k, d, :, cols] + off_buf[k, d : d + 1, cols] * in_ref[d, :, cols])
                for d in range(2)
            ]
            held = jnp.concatenate(held, axis=1)
            for part in range(2):
                some = slice(part * BLOCK // 2, (part + 1) * BLOCK // 2)
                if p % 2 == 0:
                    scales[part] = jnp.dot(
                        every_t[some],
                        hot_ref[:, p * width : (p + 2) * width],
                        preferred_element_type=F32,
                    )
                z = jnp.dot(cc[some], held, preferred_element_type=F32)
                for j in range(TILES // 2):
                    i = part * TILES // 2 + j
                    at = slice(i * TILE, (i + 1) * TILE)
                    to = slice(j * TILE, (j + 1) * TILE)
                    rows = [jnp.broadcast_to(decay[r : r + 1, at], (headdim, TILE)) for r in range(2)]
                    total = a_buf[k, at, cols] + jnp.concatenate(rows, axis=0).T * z[to, :width]
                    other = scales[part][to, p % 2 * width : (p % 2 + 1) * width]
                    total = total + other * z[to, width:]
                    half = 0.5 * gate_buf[k, at, cols].astype(F32)
                    gated = total * (half + half * jnp.tanh(half))
                    out_ref[pl.ds(pl.multiple_of(k * BLOCK + i * TILE, TILE), TILE), cols] = gated
                    squares[i] = squares[i] + gated * gated
        for i in range(TILES):
            sq_ref[k, :, i * TILE : (i + 1) * TILE] = jnp.sum(squares[i].T, axis=0, keepdims=True)


def norm_kernel(gated_ref, sq_ref, gain_hbm, out_hbm, out_buf, gain_buf, sems, gain_sem):
    blocks = out_buf.shape[0]
    gain = fetch(gain_hbm, gain_buf, gain_sem)
    copy = lambda k: pltpu.make_async_copy(
        out_buf.at[k], out_hbm.at[pl.ds(pl.multiple_of(k * BLOCK, BLOCK), BLOCK)], sems.at[k]
    )
    gain.wait()

    @pl.loop(0, blocks)
    def _(k):
        factor = lax.rsqrt(sq_ref[k] * (1.0 / INNER) + 1e-05)
        factor = jnp.broadcast_to(factor, (128, factor.shape[1])).T
        rows = pl.ds(pl.multiple_of(k * BLOCK, BLOCK), BLOCK)
        for n in range(gated_ref.shape[1] // 128):
            cols = slice(n * 128, (n + 1) * 128)
            out_buf[k, :, cols] = (gated_ref[rows, cols] * factor * gain_buf[:, cols]).astype(BF16)
        copy(k).start()

    @pl.loop(0, blocks)
    def _(k):
        copy(k).wait()


def incoming(finals, beside):
    count, mine = lax.axis_size("seq"), lax.axis_index("seq")
    rows, row, side = count // 2, mine // 2, mine % 2
    left, early = side == 0, row < rows // 2
    swap = [(i, i ^ 1) for i in range(count)]
    send = lambda value, route: lax.ppermute(value, "seq", route)
    groups = range(len(finals))
    stages = [[] for _ in groups]
    state, half = finals[0].shape[1] - 8, finals[0].shape[2] // 2
    kept, given, got1, got2 = {}, {}, {}, {}
    for g in groups:
        first, second = finals[g][:, :, :half], finals[g][:, :, half:]
        kept[g] = jnp.where(left, first, second)
        other = jnp.where(left, second, first)
        given[g] = jnp.where(early, other[0], other[1]), jnp.where(early, other[1], other[0])
        stages[g].append(given[g][0])
        got1[g] = send(given[g][0], swap)
    enter = {g: [jnp.zeros((state, half), F32)] * 2 for g in groups}
    low, high, dl, dh = {}, {}, {}, {}
    got, out1, out2 = {}, {}, {}

    def parts(g, d, arrived):
        mine_d = kept[g][d]
        lo, hi = jnp.where(left, mine_d, arrived), jnp.where(left, arrived, mine_d)
        return lo[:state], hi[:state], lo[state : state + 1], hi[state : state + 1]

    def pair(g, d, pieces):
        lo, hi, decay_lo, decay_hi = pieces
        if d == 0:
            return decay_hi * lo + hi, decay_lo * decay_hi
        return decay_lo * hi + lo, decay_lo * decay_hi

    def both(d, pieces, held):
        lo, hi, decay_lo, decay_hi = pieces
        if d == 0:
            return held, decay_lo * held + lo
        return decay_hi * held + hi, held

    def pick(flag, a, b):
        return jax.tree.map(lambda u, v: jnp.where(flag, u, v), a, b)

    token = early_token = beside(stages[0][-1])
    known = {}
    for hop in range(rows - 1):
        back = rows - 1 - hop
        route = [(2 * hop + s, 2 * hop + 2 + s) for s in range(2)]
        route += [(2 * back + s, 2 * back - 2 + s) for s in range(2)]
        for g in groups:
            if hop == 0:
                known[g] = [parts(g, d, got1[g]) for d in range(2)]
            if hop == rows // 2:
                second = [parts(g, d, got2[g] + token) for d in range(2)]
                known[g] = [pick(early, known[g][0], second[0]), pick(early, second[1], known[g][1])]
            (pf, df), (pr, dr) = pair(g, 0, known[g][0]), pair(g, 1, known[g][1])
            payload = jnp.where(row == hop, df * enter[g][0] + pf, dr * enter[g][1] + pr)
            payload = payload + token
            stages[g].append(payload)
            got[g] = send(payload, route)
        token = beside(stages[0][-1])
        for g in groups:
            if hop == 0:
                later = given[g][1] + (0.0 * got1[g] + early_token)
                got2[g] = send(later, swap)
            enter[g] = [
                jnp.where(row == hop + 1, got[g], enter[g][0]),
                jnp.where(row == back - 1, got[g], enter[g][1]),
            ]
            if hop == max(rows // 2 - 2, 0):
                ends = pick(early, both(0, known[g][0], enter[g][0]), both(1, known[g][1], enter[g][1]))
                out1[g] = (jnp.where(left, ends[0], ends[1]), send(jnp.where(left, ends[1], ends[0]), swap))
    result = []
    for g in groups:
        ends = pick(early, both(1, known[g][1], enter[g][1]), both(0, known[g][0], enter[g][0]))
        payload = jnp.where(left, ends[1], ends[0]) + token
        stages[g].append(payload)
        out2[g] = (jnp.where(left, ends[0], ends[1]), send(payload, swap))
    beside(stages[0][-1])
    for g in groups:
        whole = []
        for own, came in (out1[g], out2[g]):
            whole.append(
                jnp.concatenate([jnp.where(left, own, came), jnp.where(left, came, own)], axis=1)
            )
        result.append(
            jnp.stack([jnp.where(early, whole[0], whole[1]), jnp.where(early, whole[1], whole[0])])
        )
    return result


def shards(activations, gate_input, bmat, cmat, log_fwd, log_rev, skip, gain):
    length, channels = activations.shape
    heads = log_fwd.shape[0]
    headdim = channels // heads
    width = 2 * headdim
    state = bmat.shape[1]
    blocks = length // BLOCK
    pairs = heads // 2
    mine = pairs // GROUPS
    part = channels // GROUPS
    many = 2
    finals = []
    shared = []
    for g in range(GROUPS):
        done = list(shared)
        *shared, final = pl.pallas_call(
            functools.partial(states_kernel, headdim, bool(done)),
            grid=(mine // many,),
            in_specs=[
                pl.BlockSpec((length, many * width), lambda n, g=g: (0, g * mine // many + n)),
                pl.BlockSpec((length, state), lambda n: (0, 0)),
                pl.BlockSpec((2 * mine, length), lambda n, g=g: (g, 0)),
                pl.BlockSpec((2 * mine, length), lambda n, g=g: (g, 0)),
            ]
            + [ANY] * len(done),
            out_specs=[
                pl.BlockSpec((many, 8, length), lambda n, g=g: (g * mine // many + n, 0, 0)),
                pl.BlockSpec(
                    (blocks, 2, state, many * width),
                    lambda n, g=g: (0, 0, 0, g * mine // many + n),
                ),
                pl.BlockSpec((blocks, 8, many * width), lambda n, g=g: (0, 0, g * mine // many + n)),
                pl.BlockSpec((2, state + 8, many * width), lambda n: (0, 0, n)),
            ],
            out_shape=[
                pltpu.HBM((pairs, 8, length), F32),
                pltpu.HBM((blocks, 2, state, channels), F32),
                pltpu.HBM((blocks, 8, channels), F32),
                shape(2, state + 8, part),
            ],
            scratch_shapes=[
                pltpu.VMEM((blocks, state, BLOCK), F32),
                pltpu.VMEM((mine, blocks, 8, BLOCK), F32),
            ],
            input_output_aliases={4 + i: i for i in range(len(done))},
            compiler_params=params(24),
            name="states",
        )(*far(activations, bmat, log_fwd, log_rev, *done))
        finals.append(final)
    cum, before, off = shared
    skip_row = jnp.repeat(skip, headdim)[None]
    within = []
    some = 2
    chunks = pairs // some
    units = blocks * chunks
    cuts = [0] + [units * share // SHARES[-1] for share in SHARES]
    plan = list(zip(cuts[:-1], cuts[1:]))[::-1]

    def piece(dep):
        if not plan:
            return jnp.zeros((1, part // 2), F32)
        start, stop = plan.pop()
        block, chunk = lambda n: (start + n) // chunks, lambda n: lax.rem(start + n, chunks)
        done = list(within)
        within[:1], zero = (lambda out: ([out[0]], out[1]))(
            pl.pallas_call(
                functools.partial(within_kernel, headdim, chunks, start, bool(done)),
                grid=(stop - start,),
                in_specs=[
                    pl.BlockSpec((BLOCK, some * width), lambda n: (block(n), chunk(n))),
                    pl.BlockSpec((BLOCK, state), lambda n: (block(n), 0)),
                    pl.BlockSpec((BLOCK, state), lambda n: (block(n), 0)),
                    pl.BlockSpec((some, 8, BLOCK), lambda n: (chunk(n), 0, block(n))),
                    pl.BlockSpec((1, some * width), lambda n: (0, chunk(n))),
                    ANY,
                ]
                + [ANY] * len(done),
                out_specs=[
                    pl.BlockSpec((BLOCK, some * width), lambda n: (block(n), chunk(n))),
                    pl.BlockSpec((8, part // 2), lambda n: (0, 0)),
                ],
                out_shape=[pltpu.HBM((length, channels), F32), shape(8, part // 2)],
                scratch_shapes=[
                    pltpu.VMEM((BLOCK, BLOCK), F32),
                    pltpu.VMEM((some, TILES, 8, BLOCK), F32),
                    pltpu.VMEM((some, 8, BLOCK), F32),
                ],
                input_output_aliases={6: 0} if done else {},
                compiler_params=params(16),
                cost_estimate=pl.CostEstimate(
                    flops=2 * heads * BLOCK * BLOCK * 512,
                    bytes_accessed=6 * BLOCK * channels,
                    transcendentals=heads * BLOCK * 8,
                ),
                name="within",
            )(*far(activations, bmat, cmat, cum), skip_row, dep, *far(*done))
        )
        return zero[:1]

    enters = incoming(finals, piece)
    while plan:
        piece(finals[0])
    gated, squares = pl.pallas_call(
        functools.partial(carried_kernel, headdim),
        in_specs=[ANY] * 6 + [WHOLE],
        out_specs=[WHOLE, WHOLE],
        out_shape=[pltpu.VMEM((length, channels), F32), shape(blocks, 1, BLOCK)],
        scratch_shapes=[
            pltpu.VMEM((blocks, BLOCK, channels), F32),
            pltpu.VMEM((blocks, BLOCK, channels), BF16),
            pltpu.VMEM((blocks, BLOCK, state), BF16),
            pltpu.VMEM((blocks, pairs, 8, BLOCK), F32),
            pltpu.VMEM((blocks, 2, state, channels), F32),
            pltpu.VMEM((blocks, 8, channels), F32),
            pltpu.VMEM((16 * pairs, channels), BF16),
            pltpu.SemaphoreType.DMA((6, blocks)),
        ],
        compiler_params=pltpu.CompilerParams(vmem_limit_bytes=40 * 1024 * 1024),
        name="carried",
    )(*far(within[0], gate_input, cmat, cum, before, off), enters[0])
    step, size = 1, lax.axis_size("ch")
    while step < size:
        squares = squares + lax.ppermute(squares, "ch", [(i, i ^ step) for i in range(size)])
        step *= 2
    return pl.pallas_call(
        norm_kernel,
        in_specs=[WHOLE, WHOLE, ANY],
        out_specs=ANY,
        out_shape=shape(length, channels, dtype=BF16),
        scratch_shapes=[
            pltpu.VMEM((blocks, BLOCK, channels), BF16),
            pltpu.VMEM((1, channels), F32),
            pltpu.SemaphoreType.DMA((blocks,)),
            pltpu.SemaphoreType.DMA(()),
        ],
        compiler_params=pltpu.CompilerParams(vmem_limit_bytes=24 * 1024 * 1024),
        name="norm",
    )(*near(gated), squares, *far(gain[None]))


def solution(mesh):
    return jax.shard_map(
        shards,
        mesh=mesh,
        in_specs=(
            P("seq", "ch"),
            P("seq", "ch"),
            P("seq", None),
            P("seq", None),
            P("ch", "seq"),
            P("ch", "seq"),
            P("ch"),
            P("ch"),
        ),
        out_specs=P("seq", "ch"),
        check_vma=False,
    )
```

```python
import functools

import jax
import jax.numpy as jnp
from jax import lax
from jax.experimental import pallas as pl
from jax.experimental.pallas import tpu as pltpu
from jax.sharding import PartitionSpec as P

INNER = 4096
BLOCK = 512
TILE = 128
TILES = BLOCK // TILE
GROUPS = 1
SHARES = (2, 3, 4, 6, 8)
LOG2E = 1.4426950408889634
F32, BF16 = jnp.float32, jnp.bfloat16
ANY = pl.BlockSpec(memory_space=pl.ANY)
WHOLE = pl.BlockSpec(memory_space=pltpu.VMEM)


def shape(*dims, dtype=F32):
    return jax.ShapeDtypeStruct(dims, dtype)


def far(*values):
    return [pltpu.with_memory_space_constraint(value, pltpu.HBM) for value in values]


def near(*values):
    return [pltpu.with_memory_space_constraint(value, pltpu.VMEM) for value in values]


def params(mib):
    return pltpu.CompilerParams(
        vmem_limit_bytes=mib * 1024 * 1024, dimension_semantics=("arbitrary",)
    )


def running_sums(log, reverse):
    heads, length = log.shape
    rows = jnp.concatenate(
        [log[:, at : at + BLOCK] for at in range(0, length, BLOCK)], axis=0
    )
    high = rows.astype(BF16)
    rest = rows - high.astype(F32)
    middle = rest.astype(BF16)
    low = (rest - middle.astype(F32)).astype(BF16)
    u = lax.broadcasted_iota(jnp.int32, (BLOCK, BLOCK), 0)
    t = lax.broadcasted_iota(jnp.int32, (BLOCK, BLOCK), 1)
    taken = jnp.where(u >= t if reverse else u <= t, 1.0, 0.0).astype(BF16)
    total = [jnp.dot(part, taken, preferred_element_type=F32) for part in (low, middle, high)]
    return total[0] + total[1] + total[2]


def halves(value):
    high = value.astype(BF16)
    return jnp.concatenate([high, (value - high.astype(F32)).astype(BF16)], axis=0)


def states_kernel(headdim, chained, x_ref, b_ref, lf_ref, lr_ref, *refs):
    cum_ref, before_ref, off_ref, final_ref, bt_ref, sum_ref = refs[3 if chained else 0 :]
    step = pl.program_id(0)
    pairs, blocks = sum_ref.shape[:2]
    state = b_ref.shape[1]

    @pl.when(step == 0)
    def _():
        cf = running_sums(lf_ref[...], False) * LOG2E
        cr = running_sums(lr_ref[...], True) * LOG2E
        for k in range(blocks):
            bt_ref[k] = b_ref[k * BLOCK : (k + 1) * BLOCK].astype(F32).T
            for i in range(pairs):
                h = slice(2 * (k * pairs + i), 2 * (k * pairs + i) + 2)
                sum_ref[i, k, 0:2] = cf[h]
                sum_ref[i, k, 2:4] = cr[h]
                sum_ref[i, k, 4:8] = jnp.zeros((4, BLOCK), F32)

    first = lax.broadcasted_iota(jnp.int32, (1, 2 * headdim), 1) < headdim
    lane = lax.broadcasted_iota(jnp.int32, (state, 2 * headdim), 1)
    forward = lax.broadcasted_iota(jnp.int32, (8, 1), 0) < 2
    for one in range(cum_ref.shape[0]):
        p = step * cum_ref.shape[0] + one
        cols = slice(2 * headdim * one, 2 * headdim * (one + 1))
        fresh, decay = [], []
        for k in range(blocks):
            at = slice(k * BLOCK, (k + 1) * BLOCK)
            cum = sum_ref[p, k]
            last = jnp.where(forward, cum[:, BLOCK - 1 :], cum[:, :1])
            to_end = jnp.exp2(last - cum)
            whole = jnp.exp2(last)
            x = x_ref[at, cols]
            both = []
            for q in range(2):
                rows = [(bt_ref[k] * to_end[r : r + 1]).astype(BF16) for r in (q, 2 + q)]
                both.append(
                    jnp.dot(jnp.concatenate(rows, axis=0), x, preferred_element_type=F32)
                )
            fresh.append(
                [
                    jnp.where(
                        lane < headdim,
                        both[0][d * state : (d + 1) * state],
                        both[1][d * state : (d + 1) * state],
                    )
                    for d in range(2)
                ]
            )
            decay.append(
                [
                    jnp.where(first, whole[2 * d : 2 * d + 1], whole[2 * d + 1 : 2 * d + 2])
                    for d in range(2)
                ]
            )
            cum_ref[one, :, at] = cum
        for d in range(2):
            order = range(blocks) if d == 0 else range(blocks - 1, -1, -1)
            held = jnp.zeros_like(fresh[0][0])
            through = jnp.ones_like(decay[0][0])
            for k in order:
                before_ref[k, d, :, cols] = held
                off_ref[k, d : d + 1, cols] = through
                held = held * decay[k][d] + fresh[k][d]
                through = through * decay[k][d]
            final_ref[d, :state, cols] = held
            final_ref[d, state:, cols] = jnp.broadcast_to(through, (8, 2 * headdim))


def within_kernel(headdim, chunks, first_unit, chained, x_ref, b_ref, c_ref, cum_ref, skip_ref, dep_ref, *refs):
    out_ref, zero_ref, score_ref, row_ref, col_ref = refs[1 if chained else 0 :]
    width = 2 * headdim
    pairs = cum_ref.shape[0]
    zero_ref[...] = jnp.zeros_like(zero_ref)

    unit = first_unit + pl.program_id(0)

    @pl.when((pl.program_id(0) == 0) | (lax.rem(unit, chunks) == 0))
    def _():
        scores = lax.dot_general(
            c_ref[...], b_ref[...], (((1,), (1,)), ((), ())), preferred_element_type=F32
        )
        row = lax.broadcasted_iota(jnp.int32, (BLOCK, BLOCK), 0)
        col = lax.broadcasted_iota(jnp.int32, (BLOCK, BLOCK), 1)
        score_ref[...] = jnp.where(row == col, 2.0 * scores, scores)

    first = lax.broadcasted_iota(jnp.int32, (1, width), 1) < headdim
    lower = lax.broadcasted_iota(jnp.int32, (TILE, TILE), 0) >= lax.broadcasted_iota(
        jnp.int32, (TILE, TILE), 1
    )
    forward = lax.broadcasted_iota(jnp.int32, (8, 1), 0) < 2
    none = jnp.zeros((8, 1), F32)
    for p in range(pairs):
        cum = cum_ref[p]
        for i in range(TILES):
            lo = cum[:, i * TILE - 1 : i * TILE] if i else none
            hi = cum[:, (i + 1) * TILE : (i + 1) * TILE + 1] if i < TILES - 1 else none
            base = jnp.where(forward, lo, hi)
            row_ref[p, i] = jnp.exp2(base - cum)
            at = slice(i * TILE, (i + 1) * TILE)
            col_ref[p, :, at] = jnp.exp2(cum[:, at] - base)
        cols = slice(p * width, (p + 1) * width)
        x = x_ref[:, cols]
        parts = []
        for q in range(2):
            done = []
            for i in range(TILES):
                at = slice(i * TILE, (i + 1) * TILE)
                cf, cr = [
                    jnp.broadcast_to(col_ref[p, r : r + 1, at], (TILE, TILE)).T for r in (q, 2 + q)
                ]
                pieces = []
                for j in range(TILES):
                    to = slice(j * TILE, (j + 1) * TILE)
                    rf = row_ref[p, i, q : q + 1, to]
                    rr = row_ref[p, i, 2 + q : 3 + q, to]
                    score = score_ref[at, to]
                    if j < i:
                        weight = (score * rf) * cf
                    elif j > i:
                        weight = (score * rr) * cr
                    else:
                        weight = score * jnp.where(lower, rf * cf, rr * cr)
                    pieces.append(weight.astype(BF16))
                line = jnp.concatenate(pieces, axis=1)
                if i % 2:
                    both = jnp.concatenate([line_before, line], axis=0)
                    done.append(jnp.dot(both, x, preferred_element_type=F32))
                line_before = line
            parts.append(jnp.concatenate(done, axis=0))
        y = jnp.where(first, parts[0], parts[1])
        out_ref[:, cols] = y + skip_ref[:, cols] * x.astype(F32)


def fetch(source, target, sem):
    copy = pltpu.make_async_copy(source, target, sem)
    copy.start()
    return copy


def carried_kernel(headdim, a_hbm, gate_hbm, c_hbm, cum_hbm, before_hbm, off_hbm, in_ref, out_ref, sq_ref, *refs):
    a_buf, gate_buf, c_buf, cum_buf, before_buf, off_buf, hot_ref, sems = refs
    blocks, pairs = a_buf.shape[0], cum_buf.shape[1]
    width = 2 * headdim

    def copies(k):
        at = pl.ds(pl.multiple_of(k * BLOCK, BLOCK), BLOCK)
        pieces = [
            (before_hbm.at[k], before_buf.at[k]),
            (off_hbm.at[k], off_buf.at[k]),
            (c_hbm.at[at], c_buf.at[k]),
            (cum_hbm.at[:, :, at], cum_buf.at[k]),
            (gate_hbm.at[at], gate_buf.at[k]),
            (a_hbm.at[at], a_buf.at[k]),
        ]
        return [pltpu.make_async_copy(f, t, sems.at[n, k]) for n, (f, t) in enumerate(pieces)]

    for k in range(blocks):
        for copy in copies(k):
            copy.start()
    row = lax.broadcasted_iota(jnp.int32, (16 * pairs, 1), 0)
    row = jnp.where(row < 8 * pairs, row, row - 8 * pairs)
    lane = lax.broadcasted_iota(jnp.int32, (1, width), 1)
    for p in range(pairs):
        hot = jnp.where(row == 8 * p + 2 + jnp.where(lane < headdim, 0, 1), 1.0, 0.0)
        hot_ref[:, p * width : (p + 1) * width] = hot.astype(BF16)

    @pl.loop(0, blocks)
    def _(k):
        for copy in copies(k):
            copy.wait()
        every = jnp.exp2(cum_buf[k].reshape(8 * pairs, BLOCK))
        high = every.astype(BF16).astype(F32)
        every_t = jnp.concatenate([high, every - high], axis=0).T.astype(BF16)
        c = c_buf[k]
        cc = jnp.concatenate([c, c], axis=1)
        squares = [jnp.zeros((TILE, width), F32)] * TILES
        scales = [None, None]
        for p in range(pairs):
            cols = slice(p * width, (p + 1) * width)
            decay = every[8 * p : 8 * p + 8]
            held = [
                halves(before_buf[k, d, :, cols] + off_buf[k, d : d + 1, cols] * in_ref[d, :, cols])
                for d in range(2)
            ]
            held = jnp.concatenate(held, axis=1)
            for part in range(2):
                some = slice(part * BLOCK // 2, (part + 1) * BLOCK // 2)
                if p % 2 == 0:
                    scales[part] = jnp.dot(
                        every_t[some],
                        hot_ref[:, p * width : (p + 2) * width],
                        preferred_element_type=F32,
                    )
                z = jnp.dot(cc[some], held, preferred_element_type=F32)
                for j in range(TILES // 2):
                    i = part * TILES // 2 + j
                    at = slice(i * TILE, (i + 1) * TILE)
                    to = slice(j * TILE, (j + 1) * TILE)
                    rows = [jnp.broadcast_to(decay[r : r + 1, at], (headdim, TILE)) for r in range(2)]
                    total = a_buf[k, at, cols] + jnp.concatenate(rows, axis=0).T * z[to, :width]
                    other = scales[part][to, p % 2 * width : (p % 2 + 1) * width]
                    total = total + other * z[to, width:]
                    half = 0.5 * gate_buf[k, at, cols].astype(F32)
                    gated = total * (half + half * jnp.tanh(half))
                    out_ref[pl.ds(pl.multiple_of(k * BLOCK + i * TILE, TILE), TILE), cols] = gated
                    squares[i] = squares[i] + gated * gated
        for i in range(TILES):
            sq_ref[k, :, i * TILE : (i + 1) * TILE] = jnp.sum(squares[i].T, axis=0, keepdims=True)


def norm_kernel(gated_ref, sq_ref, gain_hbm, out_hbm, out_buf, gain_buf, sems, gain_sem):
    blocks = out_buf.shape[0]
    gain = fetch(gain_hbm, gain_buf, gain_sem)
    copy = lambda k: pltpu.make_async_copy(
        out_buf.at[k], out_hbm.at[pl.ds(pl.multiple_of(k * BLOCK, BLOCK), BLOCK)], sems.at[k]
    )
    gain.wait()

    @pl.loop(0, blocks)
    def _(k):
        factor = lax.rsqrt(sq_ref[k] * (1.0 / INNER) + 1e-05)
        factor = jnp.broadcast_to(factor, (128, factor.shape[1])).T
        rows = pl.ds(pl.multiple_of(k * BLOCK, BLOCK), BLOCK)
        for n in range(gated_ref.shape[1] // 128):
            cols = slice(n * 128, (n + 1) * 128)
            out_buf[k, :, cols] = (gated_ref[rows, cols] * factor * gain_buf[:, cols]).astype(BF16)
        copy(k).start()

    @pl.loop(0, blocks)
    def _(k):
        copy(k).wait()


def incoming(finals, beside):
    count, mine = lax.axis_size("seq"), lax.axis_index("seq")
    rows, row, side = count // 2, mine // 2, mine % 2
    left, early = side == 0, row < rows // 2
    swap = [(i, i ^ 1) for i in range(count)]
    send = lambda value, route: lax.ppermute(value, "seq", route)
    groups = range(len(finals))
    stages = [[] for _ in groups]
    state, half = finals[0].shape[1] - 8, finals[0].shape[2] // 2
    kept, given, got1, got2 = {}, {}, {}, {}
    for g in groups:
        first, second = finals[g][:, :, :half], finals[g][:, :, half:]
        kept[g] = jnp.where(left, first, second)
        other = jnp.where(left, second, first)
        given[g] = jnp.where(early, other[0], other[1]), jnp.where(early, other[1], other[0])
        stages[g].append(given[g][0])
        got1[g] = send(given[g][0], swap)
    enter = {g: [jnp.zeros((state, half), F32)] * 2 for g in groups}
    low, high, dl, dh = {}, {}, {}, {}
    got, out1, out2 = {}, {}, {}

    def parts(g, d, arrived):
        mine_d = kept[g][d]
        lo, hi = jnp.where(left, mine_d, arrived), jnp.where(left, arrived, mine_d)
        return lo[:state], hi[:state], lo[state : state + 1], hi[state : state + 1]

    def pair(g, d, pieces):
        lo, hi, decay_lo, decay_hi = pieces
        if d == 0:
            return decay_hi * lo + hi, decay_lo * decay_hi
        return decay_lo * hi + lo, decay_lo * decay_hi

    def both(d, pieces, held):
        lo, hi, decay_lo, decay_hi = pieces
        if d == 0:
            return held, decay_lo * held + lo
        return decay_hi * held + hi, held

    def pick(flag, a, b):
        return jax.tree.map(lambda u, v: jnp.where(flag, u, v), a, b)

    token = early_token = beside(stages[0][-1])
    known = {}
    for hop in range(rows - 1):
        back = rows - 1 - hop
        route = [(2 * hop + s, 2 * hop + 2 + s) for s in range(2)]
        route += [(2 * back + s, 2 * back - 2 + s) for s in range(2)]
        for g in groups:
            if hop == 0:
                known[g] = [parts(g, d, got1[g]) for d in range(2)]
            if hop == rows // 2:
                second = [parts(g, d, got2[g] + token) for d in range(2)]
                known[g] = [pick(early, known[g][0], second[0]), pick(early, second[1], known[g][1])]
            (pf, df), (pr, dr) = pair(g, 0, known[g][0]), pair(g, 1, known[g][1])
            payload = jnp.where(row == hop, df * enter[g][0] + pf, dr * enter[g][1] + pr)
            payload = payload + token
            stages[g].append(payload)
            got[g] = send(payload, route)
        token = beside(stages[0][-1])
        for g in groups:
            if hop == 0:
                later = given[g][1] + (0.0 * got1[g] + early_token)
                got2[g] = send(later, swap)
            enter[g] = [
                jnp.where(row == hop + 1, got[g], enter[g][0]),
                jnp.where(row == back - 1, got[g], enter[g][1]),
            ]
            if hop == max(rows // 2 - 2, 0):
                ends = pick(early, both(0, known[g][0], enter[g][0]), both(1, known[g][1], enter[g][1]))
                out1[g] = (jnp.where(left, ends[0], ends[1]), send(jnp.where(left, ends[1], ends[0]), swap))
    result = []
    for g in groups:
        ends = pick(early, both(1, known[g][1], enter[g][1]), both(0, known[g][0], enter[g][0]))
        payload = jnp.where(left, ends[1], ends[0]) + token
        stages[g].append(payload)
        out2[g] = (jnp.where(left, ends[0], ends[1]), send(payload, swap))
    beside(stages[0][-1])
    for g in groups:
        whole = []
        for own, came in (out1[g], out2[g]):
            whole.append(
                jnp.concatenate([jnp.where(left, own, came), jnp.where(left, came, own)], axis=1)
            )
        result.append(
            jnp.stack([jnp.where(early, whole[0], whole[1]), jnp.where(early, whole[1], whole[0])])
        )
    return result


def shards(activations, gate_input, bmat, cmat, log_fwd, log_rev, skip, gain):
    length, channels = activations.shape
    heads = log_fwd.shape[0]
    headdim = channels // heads
    width = 2 * headdim
    state = bmat.shape[1]
    blocks = length // BLOCK
    pairs = heads // 2
    mine = pairs // GROUPS
    part = channels // GROUPS
    many = 2
    finals = []
    shared = []
    for g in range(GROUPS):
        done = list(shared)
        *shared, final = pl.pallas_call(
            functools.partial(states_kernel, headdim, bool(done)),
            grid=(mine // many,),
            in_specs=[
                pl.BlockSpec((length, many * width), lambda n, g=g: (0, g * mine // many + n)),
                pl.BlockSpec((length, state), lambda n: (0, 0)),
                pl.BlockSpec((2 * mine, length), lambda n, g=g: (g, 0)),
                pl.BlockSpec((2 * mine, length), lambda n, g=g: (g, 0)),
            ]
            + [ANY] * len(done),
            out_specs=[
                pl.BlockSpec((many, 8, length), lambda n, g=g: (g * mine // many + n, 0, 0)),
                pl.BlockSpec(
                    (blocks, 2, state, many * width),
                    lambda n, g=g: (0, 0, 0, g * mine // many + n),
                ),
                pl.BlockSpec((blocks, 8, many * width), lambda n, g=g: (0, 0, g * mine // many + n)),
                pl.BlockSpec((2, state + 8, many * width), lambda n: (0, 0, n)),
            ],
            out_shape=[
                pltpu.HBM((pairs, 8, length), F32),
                pltpu.HBM((blocks, 2, state, channels), F32),
                pltpu.HBM((blocks, 8, channels), F32),
                shape(2, state + 8, part),
            ],
            scratch_shapes=[
                pltpu.VMEM((blocks, state, BLOCK), F32),
                pltpu.VMEM((mine, blocks, 8, BLOCK), F32),
            ],
            input_output_aliases={4 + i: i for i in range(len(done))},
            compiler_params=params(24),
            name="states",
        )(*far(activations, bmat, log_fwd, log_rev, *done))
        finals.append(final)
    cum, before, off = shared
    skip_row = jnp.repeat(skip, headdim)[None]
    within = []
    some = 4
    chunks = pairs // some
    units = blocks * chunks
    cuts = [0] + [units * share // SHARES[-1] for share in SHARES]
    plan = list(zip(cuts[:-1], cuts[1:]))[::-1]

    def piece(dep):
        if not plan:
            return jnp.zeros((1, part // 2), F32)
        start, stop = plan.pop()
        block, chunk = lambda n: (start + n) // chunks, lambda n: lax.rem(start + n, chunks)
        done = list(within)
        within[:1], zero = (lambda out: ([out[0]], out[1]))(
            pl.pallas_call(
                functools.partial(within_kernel, headdim, chunks, start, bool(done)),
                grid=(stop - start,),
                in_specs=[
                    pl.BlockSpec((BLOCK, some * width), lambda n: (block(n), chunk(n))),
                    pl.BlockSpec((BLOCK, state), lambda n: (block(n), 0)),
                    pl.BlockSpec((BLOCK, state), lambda n: (block(n), 0)),
                    pl.BlockSpec((some, 8, BLOCK), lambda n: (chunk(n), 0, block(n))),
                    pl.BlockSpec((1, some * width), lambda n: (0, chunk(n))),
                    ANY,
                ]
                + [ANY] * len(done),
                out_specs=[
                    pl.BlockSpec((BLOCK, some * width), lambda n: (block(n), chunk(n))),
                    pl.BlockSpec((8, part // 2), lambda n: (0, 0)),
                ],
                out_shape=[pltpu.HBM((length, channels), F32), shape(8, part // 2)],
                scratch_shapes=[
                    pltpu.VMEM((BLOCK, BLOCK), F32),
                    pltpu.VMEM((some, TILES, 8, BLOCK), F32),
                    pltpu.VMEM((some, 8, BLOCK), F32),
                ],
                input_output_aliases={6: 0} if done else {},
                compiler_params=params(16),
                cost_estimate=pl.CostEstimate(
                    flops=2 * heads * BLOCK * BLOCK * 512,
                    bytes_accessed=6 * BLOCK * channels,
                    transcendentals=heads * BLOCK * 8,
                ),
                name="within",
            )(*far(activations, bmat, cmat, cum), skip_row, dep, *far(*done))
        )
        return zero[:1]

    enters = incoming(finals, piece)
    while plan:
        piece(finals[0])
    gated, squares = pl.pallas_call(
        functools.partial(carried_kernel, headdim),
        in_specs=[ANY] * 6 + [WHOLE],
        out_specs=[WHOLE, WHOLE],
        out_shape=[pltpu.VMEM((length, channels), F32), shape(blocks, 1, BLOCK)],
        scratch_shapes=[
            pltpu.VMEM((blocks, BLOCK, channels), F32),
            pltpu.VMEM((blocks, BLOCK, channels), BF16),
            pltpu.VMEM((blocks, BLOCK, state), BF16),
            pltpu.VMEM((blocks, pairs, 8, BLOCK), F32),
            pltpu.VMEM((blocks, 2, state, channels), F32),
            pltpu.VMEM((blocks, 8, channels), F32),
            pltpu.VMEM((16 * pairs, channels), BF16),
            pltpu.SemaphoreType.DMA((6, blocks)),
        ],
        compiler_params=pltpu.CompilerParams(vmem_limit_bytes=40 * 1024 * 1024),
        name="carried",
    )(*far(within[0], gate_input, cmat, cum, before, off), enters[0])
    step, size = 1, lax.axis_size("ch")
    while step < size:
        squares = squares + lax.ppermute(squares, "ch", [(i, i ^ step) for i in range(size)])
        step *= 2
    return pl.pallas_call(
        norm_kernel,
        in_specs=[WHOLE, WHOLE, ANY],
        out_specs=ANY,
        out_shape=shape(length, channels, dtype=BF16),
        scratch_shapes=[
            pltpu.VMEM((blocks, BLOCK, channels), BF16),
            pltpu.VMEM((1, channels), F32),
            pltpu.SemaphoreType.DMA((blocks,)),
            pltpu.SemaphoreType.DMA(()),
        ],
        compiler_params=pltpu.CompilerParams(vmem_limit_bytes=24 * 1024 * 1024),
        name="norm",
    )(*near(gated), squares, *far(gain[None]))


def solution(mesh):
    return jax.shard_map(
        shards,
        mesh=mesh,
        in_specs=(
            P("seq", "ch"),
            P("seq", "ch"),
            P("seq", None),
            P("seq", None),
            P("ch", "seq"),
            P("ch", "seq"),
            P("ch"),
            P("ch"),
        ),
        out_specs=P("seq", "ch"),
        check_vma=False,
    )
```

```python
import functools

import jax
import jax.numpy as jnp
from jax import lax
from jax.experimental import pallas as pl
from jax.experimental.pallas import tpu as pltpu
from jax.sharding import PartitionSpec as P

INNER = 4096
BLOCK = 512
TILE = 128
TILES = BLOCK // TILE
GROUPS = 1
SHARES = (2, 3, 4, 6, 8)
LOG2E = 1.4426950408889634
F32, BF16 = jnp.float32, jnp.bfloat16
ANY = pl.BlockSpec(memory_space=pl.ANY)
WHOLE = pl.BlockSpec(memory_space=pltpu.VMEM)


def shape(*dims, dtype=F32):
    return jax.ShapeDtypeStruct(dims, dtype)


def far(*values):
    return [pltpu.with_memory_space_constraint(value, pltpu.HBM) for value in values]


def near(*values):
    return [pltpu.with_memory_space_constraint(value, pltpu.VMEM) for value in values]


def params(mib):
    return pltpu.CompilerParams(
        vmem_limit_bytes=mib * 1024 * 1024, dimension_semantics=("arbitrary",)
    )


def running_sums(log, reverse):
    heads, length = log.shape
    rows = jnp.concatenate(
        [log[:, at : at + BLOCK] for at in range(0, length, BLOCK)], axis=0
    )
    high = rows.astype(BF16)
    rest = rows - high.astype(F32)
    middle = rest.astype(BF16)
    low = (rest - middle.astype(F32)).astype(BF16)
    u = lax.broadcasted_iota(jnp.int32, (BLOCK, BLOCK), 0)
    t = lax.broadcasted_iota(jnp.int32, (BLOCK, BLOCK), 1)
    taken = jnp.where(u >= t if reverse else u <= t, 1.0, 0.0).astype(BF16)
    total = [jnp.dot(part, taken, preferred_element_type=F32) for part in (low, middle, high)]
    return total[0] + total[1] + total[2]


def halves(value):
    high = value.astype(BF16)
    return jnp.concatenate([high, (value - high.astype(F32)).astype(BF16)], axis=0)


def states_kernel(headdim, chained, x_ref, b_ref, lf_ref, lr_ref, *refs):
    cum_ref, before_ref, off_ref, final_ref, bt_ref, sum_ref = refs[3 if chained else 0 :]
    step = pl.program_id(0)
    pairs, blocks = sum_ref.shape[:2]
    state = b_ref.shape[1]

    @pl.when(step == 0)
    def _():
        cf = running_sums(lf_ref[...], False) * LOG2E
        cr = running_sums(lr_ref[...], True) * LOG2E
        for k in range(blocks):
            bt_ref[k] = b_ref[k * BLOCK : (k + 1) * BLOCK].astype(F32).T
            for i in range(pairs):
                h = slice(2 * (k * pairs + i), 2 * (k * pairs + i) + 2)
                sum_ref[i, k, 0:2] = cf[h]
                sum_ref[i, k, 2:4] = cr[h]
                sum_ref[i, k, 4:8] = jnp.zeros((4, BLOCK), F32)

    first = lax.broadcasted_iota(jnp.int32, (1, 2 * headdim), 1) < headdim
    lane = lax.broadcasted_iota(jnp.int32, (state, 2 * headdim), 1)
    forward = lax.broadcasted_iota(jnp.int32, (8, 1), 0) < 2
    for one in range(cum_ref.shape[0]):
        p = step * cum_ref.shape[0] + one
        cols = slice(2 * headdim * one, 2 * headdim * (one + 1))
        fresh, decay = [], []
        for k in range(blocks):
            at = slice(k * BLOCK, (k + 1) * BLOCK)
            cum = sum_ref[p, k]
            last = jnp.where(forward, cum[:, BLOCK - 1 :], cum[:, :1])
            to_end = jnp.exp2(last - cum)
            whole = jnp.exp2(last)
            x = x_ref[at, cols]
            both = []
            for q in range(2):
                rows = [(bt_ref[k] * to_end[r : r + 1]).astype(BF16) for r in (q, 2 + q)]
                both.append(
                    jnp.dot(jnp.concatenate(rows, axis=0), x, preferred_element_type=F32)
                )
            fresh.append(
                [
                    jnp.where(
                        lane < headdim,
                        both[0][d * state : (d + 1) * state],
                        both[1][d * state : (d + 1) * state],
                    )
                    for d in range(2)
                ]
            )
            decay.append(
                [
                    jnp.where(first, whole[2 * d : 2 * d + 1], whole[2 * d + 1 : 2 * d + 2])
                    for d in range(2)
                ]
            )
            cum_ref[one, :, at] = cum
        for d in range(2):
            order = range(blocks) if d == 0 else range(blocks - 1, -1, -1)
            held = jnp.zeros_like(fresh[0][0])
            through = jnp.ones_like(decay[0][0])
            for k in order:
                before_ref[k, d, :, cols] = held
                off_ref[k, d : d + 1, cols] = through
                held = held * decay[k][d] + fresh[k][d]
                through = through * decay[k][d]
            final_ref[d, :state, cols] = held
            final_ref[d, state:, cols] = jnp.broadcast_to(through, (8, 2 * headdim))


def within_kernel(headdim, chunks, first_unit, chained, x_ref, b_ref, c_ref, cum_ref, skip_ref, dep_ref, *refs):
    out_ref, zero_ref, score_ref, row_ref, col_ref = refs[1 if chained else 0 :]
    width = 2 * headdim
    pairs = cum_ref.shape[0]
    zero_ref[...] = jnp.zeros_like(zero_ref)

    unit = first_unit + pl.program_id(0)

    @pl.when((pl.program_id(0) == 0) | (lax.rem(unit, chunks) == 0))
    def _():
        scores = lax.dot_general(
            c_ref[...], b_ref[...], (((1,), (1,)), ((), ())), preferred_element_type=F32
        )
        row = lax.broadcasted_iota(jnp.int32, (BLOCK, BLOCK), 0)
        col = lax.broadcasted_iota(jnp.int32, (BLOCK, BLOCK), 1)
        score_ref[...] = jnp.where(row == col, 2.0 * scores, scores)

    first = lax.broadcasted_iota(jnp.int32, (1, width), 1) < headdim
    lower = lax.broadcasted_iota(jnp.int32, (TILE, TILE), 0) >= lax.broadcasted_iota(
        jnp.int32, (TILE, TILE), 1
    )
    forward = lax.broadcasted_iota(jnp.int32, (8, 1), 0) < 2
    none = jnp.zeros((8, 1), F32)
    for p in range(pairs):
        cum = cum_ref[p]
        for i in range(TILES):
            lo = cum[:, i * TILE - 1 : i * TILE] if i else none
            hi = cum[:, (i + 1) * TILE : (i + 1) * TILE + 1] if i < TILES - 1 else none
            base = jnp.where(forward, lo, hi)
            row_ref[p, i] = jnp.exp2(base - cum)
            at = slice(i * TILE, (i + 1) * TILE)
            col_ref[p, :, at] = jnp.exp2(cum[:, at] - base)
        cols = slice(p * width, (p + 1) * width)
        x = x_ref[:, cols]
        parts = []
        for q in range(2):
            done = []
            for i in range(TILES):
                at = slice(i * TILE, (i + 1) * TILE)
                cf, cr = [
                    jnp.broadcast_to(col_ref[p, r : r + 1, at], (TILE, TILE)).T for r in (q, 2 + q)
                ]
                pieces = []
                for j in range(TILES):
                    to = slice(j * TILE, (j + 1) * TILE)
                    rf = row_ref[p, i, q : q + 1, to]
                    rr = row_ref[p, i, 2 + q : 3 + q, to]
                    score = score_ref[at, to]
                    if j < i:
                        weight = (score * rf) * cf
                    elif j > i:
                        weight = (score * rr) * cr
                    else:
                        weight = score * jnp.where(lower, rf * cf, rr * cr)
                    pieces.append(weight.astype(BF16))
                line = jnp.concatenate(pieces, axis=1)
                if i % 2:
                    both = jnp.concatenate([line_before, line], axis=0)
                    done.append(jnp.dot(both, x, preferred_element_type=F32))
                line_before = line
            parts.append(jnp.concatenate(done, axis=0))
        y = jnp.where(first, parts[0], parts[1])
        out_ref[:, cols] = y + skip_ref[:, cols] * x.astype(F32)


def fetch(source, target, sem):
    copy = pltpu.make_async_copy(source, target, sem)
    copy.start()
    return copy


def carried_kernel(headdim, a_hbm, gate_hbm, c_hbm, cum_hbm, before_hbm, off_hbm, in_ref, out_ref, sq_ref, *refs):
    a_buf, gate_buf, c_buf, cum_buf, before_buf, off_buf, hot_ref, sems = refs
    blocks, pairs = a_buf.shape[0], cum_buf.shape[1]
    width = 2 * headdim

    def copies(k):
        at = pl.ds(k * BLOCK, BLOCK)
        pieces = [
            (before_hbm.at[k], before_buf.at[k]),
            (off_hbm.at[k], off_buf.at[k]),
            (c_hbm.at[at], c_buf.at[k]),
            (cum_hbm.at[:, :, at], cum_buf.at[k]),
            (gate_hbm.at[at], gate_buf.at[k]),
            (a_hbm.at[at], a_buf.at[k]),
        ]
        return [pltpu.make_async_copy(f, t, sems.at[n, k]) for n, (f, t) in enumerate(pieces)]

    for k in range(blocks):
        for copy in copies(k):
            copy.start()
    row = lax.broadcasted_iota(jnp.int32, (16 * pairs, 1), 0)
    row = jnp.where(row < 8 * pairs, row, row - 8 * pairs)
    lane = lax.broadcasted_iota(jnp.int32, (1, width), 1)
    for p in range(pairs):
        hot = jnp.where(row == 8 * p + 2 + jnp.where(lane < headdim, 0, 1), 1.0, 0.0)
        hot_ref[:, p * width : (p + 1) * width] = hot.astype(BF16)

    for k in range(blocks):
        for copy in copies(k):
            copy.wait()
        every = jnp.exp2(cum_buf[k].reshape(8 * pairs, BLOCK))
        high = every.astype(BF16).astype(F32)
        every_t = jnp.concatenate([high, every - high], axis=0).T.astype(BF16)
        c = c_buf[k]
        cc = jnp.concatenate([c, c], axis=1)
        squares = [jnp.zeros((TILE, width), F32)] * TILES
        scales = [None, None]
        for p in range(pairs):
            cols = slice(p * width, (p + 1) * width)
            decay = every[8 * p : 8 * p + 8]
            held = [
                halves(before_buf[k, d, :, cols] + off_buf[k, d : d + 1, cols] * in_ref[d, :, cols])
                for d in range(2)
            ]
            held = jnp.concatenate(held, axis=1)
            for part in range(2):
                some = slice(part * BLOCK // 2, (part + 1) * BLOCK // 2)
                if p % 2 == 0:
                    scales[part] = jnp.dot(
                        every_t[some],
                        hot_ref[:, p * width : (p + 2) * width],
                        preferred_element_type=F32,
                    )
                z = jnp.dot(cc[some], held, preferred_element_type=F32)
                for j in range(TILES // 2):
                    i = part * TILES // 2 + j
                    at = slice(i * TILE, (i + 1) * TILE)
                    to = slice(j * TILE, (j + 1) * TILE)
                    rows = [jnp.broadcast_to(decay[r : r + 1, at], (headdim, TILE)) for r in range(2)]
                    total = a_buf[k, at, cols] + jnp.concatenate(rows, axis=0).T * z[to, :width]
                    other = scales[part][to, p % 2 * width : (p % 2 + 1) * width]
                    total = total + other * z[to, width:]
                    half = 0.5 * gate_buf[k, at, cols].astype(F32)
                    gated = total * (half + half * jnp.tanh(half))
                    out_ref[pl.ds(k * BLOCK + i * TILE, TILE), cols] = gated
                    squares[i] = squares[i] + gated * gated
        for i in range(TILES):
            sq_ref[k, :, i * TILE : (i + 1) * TILE] = jnp.sum(squares[i].T, axis=0, keepdims=True)


def norm_kernel(gated_ref, sq_ref, gain_hbm, out_hbm, out_buf, gain_buf, sems, gain_sem):
    fetch(gain_hbm, gain_buf, gain_sem).wait()
    chunk = out_buf.shape[1]
    copies = []
    for k in range(out_buf.shape[0]):
        start = k * chunk % BLOCK
        squares = sq_ref[k * chunk // BLOCK, :, start : start + chunk]
        factor = lax.rsqrt(squares * (1.0 / INNER) + 1e-05)
        factor = jnp.broadcast_to(factor, (128, chunk)).T
        rows = pl.ds(k * chunk, chunk)
        for n in range(gated_ref.shape[1] // 128):
            cols = slice(n * 128, (n + 1) * 128)
            out_buf[k, :, cols] = (gated_ref[rows, cols] * factor * gain_buf[:, cols]).astype(BF16)
        copies.append(fetch(out_buf.at[k], out_hbm.at[rows], sems.at[k]))
    for copy in copies:
        copy.wait()


def incoming(finals, beside):
    count, mine = lax.axis_size("seq"), lax.axis_index("seq")
    rows, row, side = count // 2, mine // 2, mine % 2
    left, early = side == 0, row < rows // 2
    swap = [(i, i ^ 1) for i in range(count)]
    send = lambda value, route: lax.ppermute(value, "seq", route)
    groups = range(len(finals))
    stages = [[] for _ in groups]
    state, half = finals[0].shape[1] - 8, finals[0].shape[2] // 2
    kept, given, got1, got2 = {}, {}, {}, {}
    for g in groups:
        first, second = finals[g][:, :, :half], finals[g][:, :, half:]
        kept[g] = jnp.where(left, first, second)
        other = jnp.where(left, second, first)
        given[g] = jnp.where(early, other[0], other[1]), jnp.where(early, other[1], other[0])
        stages[g].append(given[g][0])
        got1[g] = send(given[g][0], swap)
    enter = {g: [jnp.zeros((state, half), F32)] * 2 for g in groups}
    low, high, dl, dh = {}, {}, {}, {}
    got, out1, out2 = {}, {}, {}

    def parts(g, d, arrived):
        mine_d = kept[g][d]
        lo, hi = jnp.where(left, mine_d, arrived), jnp.where(left, arrived, mine_d)
        return lo[:state], hi[:state], lo[state : state + 1], hi[state : state + 1]

    def pair(g, d, pieces):
        lo, hi, decay_lo, decay_hi = pieces
        if d == 0:
            return decay_hi * lo + hi, decay_lo * decay_hi
        return decay_lo * hi + lo, decay_lo * decay_hi

    def both(d, pieces, held):
        lo, hi, decay_lo, decay_hi = pieces
        if d == 0:
            return held, decay_lo * held + lo
        return decay_hi * held + hi, held

    def pick(flag, a, b):
        return jax.tree.map(lambda u, v: jnp.where(flag, u, v), a, b)

    token = early_token = beside(stages[0][-1])
    known = {}
    for hop in range(rows - 1):
        back = rows - 1 - hop
        route = [(2 * hop + s, 2 * hop + 2 + s) for s in range(2)]
        route += [(2 * back + s, 2 * back - 2 + s) for s in range(2)]
        for g in groups:
            if hop == 0:
                known[g] = [parts(g, d, got1[g]) for d in range(2)]
            if hop == rows // 2:
                second = [parts(g, d, got2[g] + token) for d in range(2)]
                known[g] = [pick(early, known[g][0], second[0]), pick(early, second[1], known[g][1])]
            (pf, df), (pr, dr) = pair(g, 0, known[g][0]), pair(g, 1, known[g][1])
            payload = jnp.where(row == hop, df * enter[g][0] + pf, dr * enter[g][1] + pr)
            payload = payload + token
            stages[g].append(payload)
            got[g] = send(payload, route)
        token = beside(stages[0][-1])
        for g in groups:
            if hop == 0:
                later = given[g][1] + (0.0 * got1[g] + early_token)
                got2[g] = send(later, swap)
            enter[g] = [
                jnp.where(row == hop + 1, got[g], enter[g][0]),
                jnp.where(row == back - 1, got[g], enter[g][1]),
            ]
            if hop == max(rows // 2 - 2, 0):
                ends = pick(early, both(0, known[g][0], enter[g][0]), both(1, known[g][1], enter[g][1]))
                out1[g] = (jnp.where(left, ends[0], ends[1]), send(jnp.where(left, ends[1], ends[0]), swap))
    result = []
    for g in groups:
        ends = pick(early, both(1, known[g][1], enter[g][1]), both(0, known[g][0], enter[g][0]))
        payload = jnp.where(left, ends[1], ends[0]) + token
        stages[g].append(payload)
        out2[g] = (jnp.where(left, ends[0], ends[1]), send(payload, swap))
    beside(stages[0][-1])
    for g in groups:
        whole = []
        for own, came in (out1[g], out2[g]):
            whole.append(
                jnp.concatenate([jnp.where(left, own, came), jnp.where(left, came, own)], axis=1)
            )
        result.append(
            jnp.stack([jnp.where(early, whole[0], whole[1]), jnp.where(early, whole[1], whole[0])])
        )
    return result


def shards(activations, gate_input, bmat, cmat, log_fwd, log_rev, skip, gain):
    length, channels = activations.shape
    heads = log_fwd.shape[0]
    headdim = channels // heads
    width = 2 * headdim
    state = bmat.shape[1]
    blocks = length // BLOCK
    pairs = heads // 2
    mine = pairs // GROUPS
    part = channels // GROUPS
    many = 2
    finals = []
    shared = []
    for g in range(GROUPS):
        done = list(shared)
        *shared, final = pl.pallas_call(
            functools.partial(states_kernel, headdim, bool(done)),
            grid=(mine // many,),
            in_specs=[
                pl.BlockSpec((length, many * width), lambda n, g=g: (0, g * mine // many + n)),
                pl.BlockSpec((length, state), lambda n: (0, 0)),
                pl.BlockSpec((2 * mine, length), lambda n, g=g: (g, 0)),
                pl.BlockSpec((2 * mine, length), lambda n, g=g: (g, 0)),
            ]
            + [ANY] * len(done),
            out_specs=[
                pl.BlockSpec((many, 8, length), lambda n, g=g: (g * mine // many + n, 0, 0)),
                pl.BlockSpec(
                    (blocks, 2, state, many * width),
                    lambda n, g=g: (0, 0, 0, g * mine // many + n),
                ),
                pl.BlockSpec((blocks, 8, many * width), lambda n, g=g: (0, 0, g * mine // many + n)),
                pl.BlockSpec((2, state + 8, many * width), lambda n: (0, 0, n)),
            ],
            out_shape=[
                pltpu.HBM((pairs, 8, length), F32),
                pltpu.HBM((blocks, 2, state, channels), F32),
                pltpu.HBM((blocks, 8, channels), F32),
                shape(2, state + 8, part),
            ],
            scratch_shapes=[
                pltpu.VMEM((blocks, state, BLOCK), F32),
                pltpu.VMEM((mine, blocks, 8, BLOCK), F32),
            ],
            input_output_aliases={4 + i: i for i in range(len(done))},
            compiler_params=params(24),
            name="states",
        )(*far(activations, bmat, log_fwd, log_rev, *done))
        finals.append(final)
    cum, before, off = shared
    skip_row = jnp.repeat(skip, headdim)[None]
    within = []
    some = 4
    chunks = pairs // some
    units = blocks * chunks
    cuts = [0] + [units * share // SHARES[-1] for share in SHARES]
    plan = list(zip(cuts[:-1], cuts[1:]))[::-1]

    def piece(dep):
        if not plan:
            return jnp.zeros((1, part // 2), F32)
        start, stop = plan.pop()
        block, chunk = lambda n: (start + n) // chunks, lambda n: lax.rem(start + n, chunks)
        done = list(within)
        within[:1], zero = (lambda out: ([out[0]], out[1]))(
            pl.pallas_call(
                functools.partial(within_kernel, headdim, chunks, start, bool(done)),
                grid=(stop - start,),
                in_specs=[
                    pl.BlockSpec((BLOCK, some * width), lambda n: (block(n), chunk(n))),
                    pl.BlockSpec((BLOCK, state), lambda n: (block(n), 0)),
                    pl.BlockSpec((BLOCK, state), lambda n: (block(n), 0)),
                    pl.BlockSpec((some, 8, BLOCK), lambda n: (chunk(n), 0, block(n))),
                    pl.BlockSpec((1, some * width), lambda n: (0, chunk(n))),
                    ANY,
                ]
                + [ANY] * len(done),
                out_specs=[
                    pl.BlockSpec((BLOCK, some * width), lambda n: (block(n), chunk(n))),
                    pl.BlockSpec((8, part // 2), lambda n: (0, 0)),
                ],
                out_shape=[pltpu.HBM((length, channels), F32), shape(8, part // 2)],
                scratch_shapes=[
                    pltpu.VMEM((BLOCK, BLOCK), F32),
                    pltpu.VMEM((some, TILES, 8, BLOCK), F32),
                    pltpu.VMEM((some, 8, BLOCK), F32),
                ],
                input_output_aliases={6: 0} if done else {},
                compiler_params=params(16),
                cost_estimate=pl.CostEstimate(
                    flops=2 * heads * BLOCK * BLOCK * 512,
                    bytes_accessed=6 * BLOCK * channels,
                    transcendentals=heads * BLOCK * 8,
                ),
                name="within",
            )(*far(activations, bmat, cmat, cum), skip_row, dep, *far(*done))
        )
        return zero[:1]

    enters = incoming(finals, piece)
    while plan:
        piece(finals[0])
    gated, squares = pl.pallas_call(
        functools.partial(carried_kernel, headdim),
        in_specs=[ANY] * 6 + [WHOLE],
        out_specs=[WHOLE, WHOLE],
        out_shape=[pltpu.VMEM((length, channels), F32), shape(blocks, 1, BLOCK)],
        scratch_shapes=[
            pltpu.VMEM((blocks, BLOCK, channels), F32),
            pltpu.VMEM((blocks, BLOCK, channels), BF16),
            pltpu.VMEM((blocks, BLOCK, state), BF16),
            pltpu.VMEM((blocks, pairs, 8, BLOCK), F32),
            pltpu.VMEM((blocks, 2, state, channels), F32),
            pltpu.VMEM((blocks, 8, channels), F32),
            pltpu.VMEM((16 * pairs, channels), BF16),
            pltpu.SemaphoreType.DMA((6, blocks)),
        ],
        compiler_params=pltpu.CompilerParams(vmem_limit_bytes=40 * 1024 * 1024),
        name="carried",
    )(*far(within[0], gate_input, cmat, cum, before, off), enters[0])
    step, size = 1, lax.axis_size("ch")
    while step < size:
        squares = squares + lax.ppermute(squares, "ch", [(i, i ^ step) for i in range(size)])
        step *= 2
    return pl.pallas_call(
        norm_kernel,
        in_specs=[WHOLE, WHOLE, ANY],
        out_specs=ANY,
        out_shape=shape(length, channels, dtype=BF16),
        scratch_shapes=[
            pltpu.VMEM((2 * blocks, BLOCK // 2, channels), BF16),
            pltpu.VMEM((1, channels), F32),
            pltpu.SemaphoreType.DMA((2 * blocks,)),
            pltpu.SemaphoreType.DMA(()),
        ],
        compiler_params=pltpu.CompilerParams(vmem_limit_bytes=24 * 1024 * 1024),
        name="norm",
    )(*near(gated), squares, *far(gain[None]))


def solution(mesh):
    return jax.shard_map(
        shards,
        mesh=mesh,
        in_specs=(
            P("seq", "ch"),
            P("seq", "ch"),
            P("seq", None),
            P("seq", None),
            P("ch", "seq"),
            P("ch", "seq"),
            P("ch"),
            P("ch"),
        ),
        out_specs=P("seq", "ch"),
        check_vma=False,
    )
```

```python
import functools

import jax
import jax.numpy as jnp
from jax import lax
from jax.experimental import pallas as pl
from jax.experimental.pallas import tpu as pltpu
from jax.sharding import PartitionSpec as P

INNER = 4096
BLOCK = 512
TILE = 128
TILES = BLOCK // TILE
GROUPS = 1
SHARES = (2, 3, 4, 6, 8)
LOG2E = 1.4426950408889634
F32, BF16 = jnp.float32, jnp.bfloat16
ANY = pl.BlockSpec(memory_space=pl.ANY)
WHOLE = pl.BlockSpec(memory_space=pltpu.VMEM)


def shape(*dims, dtype=F32):
    return jax.ShapeDtypeStruct(dims, dtype)


def far(*values):
    return [pltpu.with_memory_space_constraint(value, pltpu.HBM) for value in values]


def near(*values):
    return [pltpu.with_memory_space_constraint(value, pltpu.VMEM) for value in values]


def params(mib):
    return pltpu.CompilerParams(
        vmem_limit_bytes=mib * 1024 * 1024, dimension_semantics=("arbitrary",)
    )


def running_sums(log, reverse):
    heads, length = log.shape
    rows = jnp.concatenate(
        [log[:, at : at + BLOCK] for at in range(0, length, BLOCK)], axis=0
    )
    high = rows.astype(BF16)
    rest = rows - high.astype(F32)
    middle = rest.astype(BF16)
    low = (rest - middle.astype(F32)).astype(BF16)
    u = lax.broadcasted_iota(jnp.int32, (BLOCK, BLOCK), 0)
    t = lax.broadcasted_iota(jnp.int32, (BLOCK, BLOCK), 1)
    taken = jnp.where(u >= t if reverse else u <= t, 1.0, 0.0).astype(BF16)
    total = [jnp.dot(part, taken, preferred_element_type=F32) for part in (low, middle, high)]
    return total[0] + total[1] + total[2]


def halves(value):
    high = value.astype(BF16)
    return jnp.concatenate([high, (value - high.astype(F32)).astype(BF16)], axis=0)


def states_kernel(headdim, chained, x_ref, b_ref, lf_ref, lr_ref, *refs):
    cum_ref, before_ref, off_ref, final_ref, bt_ref, sum_ref = refs[3 if chained else 0 :]
    step = pl.program_id(0)
    pairs, blocks = sum_ref.shape[:2]
    state = b_ref.shape[1]

    @pl.when(step == 0)
    def _():
        cf = running_sums(lf_ref[...], False) * LOG2E
        cr = running_sums(lr_ref[...], True) * LOG2E
        for k in range(blocks):
            bt_ref[k] = b_ref[k * BLOCK : (k + 1) * BLOCK].astype(F32).T
            for i in range(pairs):
                h = slice(2 * (k * pairs + i), 2 * (k * pairs + i) + 2)
                sum_ref[i, k, 0:2] = cf[h]
                sum_ref[i, k, 2:4] = cr[h]
                sum_ref[i, k, 4:8] = jnp.zeros((4, BLOCK), F32)

    first = lax.broadcasted_iota(jnp.int32, (1, 2 * headdim), 1) < headdim
    lane = lax.broadcasted_iota(jnp.int32, (state, 2 * headdim), 1)
    forward = lax.broadcasted_iota(jnp.int32, (8, 1), 0) < 2
    for one in range(cum_ref.shape[0]):
        p = step * cum_ref.shape[0] + one
        cols = slice(2 * headdim * one, 2 * headdim * (one + 1))
        fresh, decay = [], []
        for k in range(blocks):
            at = slice(k * BLOCK, (k + 1) * BLOCK)
            cum = sum_ref[p, k]
            last = jnp.where(forward, cum[:, BLOCK - 1 :], cum[:, :1])
            to_end = jnp.exp2(last - cum)
            whole = jnp.exp2(last)
            x = x_ref[at, cols]
            both = []
            for q in range(2):
                rows = [(bt_ref[k] * to_end[r : r + 1]).astype(BF16) for r in (q, 2 + q)]
                both.append(
                    jnp.dot(jnp.concatenate(rows, axis=0), x, preferred_element_type=F32)
                )
            fresh.append(
                [
                    jnp.where(
                        lane < headdim,
                        both[0][d * state : (d + 1) * state],
                        both[1][d * state : (d + 1) * state],
                    )
                    for d in range(2)
                ]
            )
            decay.append(
                [
                    jnp.where(first, whole[2 * d : 2 * d + 1], whole[2 * d + 1 : 2 * d + 2])
                    for d in range(2)
                ]
            )
            cum_ref[one, :, at] = cum
        for d in range(2):
            order = range(blocks) if d == 0 else range(blocks - 1, -1, -1)
            held = jnp.zeros_like(fresh[0][0])
            through = jnp.ones_like(decay[0][0])
            for k in order:
                before_ref[k, d, :, cols] = held
                off_ref[k, d : d + 1, cols] = through
                held = held * decay[k][d] + fresh[k][d]
                through = through * decay[k][d]
            final_ref[d, :state, cols] = held
            final_ref[d, state:, cols] = jnp.broadcast_to(through, (8, 2 * headdim))


def within_kernel(headdim, chunks, first_unit, chained, x_ref, b_ref, c_ref, cum_ref, skip_ref, dep_ref, *refs):
    out_ref, zero_ref, score_ref, row_ref, col_ref = refs[1 if chained else 0 :]
    width = 2 * headdim
    pairs = cum_ref.shape[0]
    zero_ref[...] = jnp.zeros_like(zero_ref)

    unit = first_unit + pl.program_id(0)

    @pl.when((pl.program_id(0) == 0) | (lax.rem(unit, chunks) == 0))
    def _():
        scores = lax.dot_general(
            c_ref[...], b_ref[...], (((1,), (1,)), ((), ())), preferred_element_type=F32
        )
        row = lax.broadcasted_iota(jnp.int32, (BLOCK, BLOCK), 0)
        col = lax.broadcasted_iota(jnp.int32, (BLOCK, BLOCK), 1)
        score_ref[...] = jnp.where(row == col, 2.0 * scores, scores)

    first = lax.broadcasted_iota(jnp.int32, (1, width), 1) < headdim
    lower = lax.broadcasted_iota(jnp.int32, (TILE, TILE), 0) >= lax.broadcasted_iota(
        jnp.int32, (TILE, TILE), 1
    )
    forward = lax.broadcasted_iota(jnp.int32, (8, 1), 0) < 2
    none = jnp.zeros((8, 1), F32)
    for p in range(pairs):
        cum = cum_ref[p]
        for i in range(TILES):
            lo = cum[:, i * TILE - 1 : i * TILE] if i else none
            hi = cum[:, (i + 1) * TILE : (i + 1) * TILE + 1] if i < TILES - 1 else none
            base = jnp.where(forward, lo, hi)
            row_ref[p, i] = jnp.exp2(base - cum)
            at = slice(i * TILE, (i + 1) * TILE)
            col_ref[p, :, at] = jnp.exp2(cum[:, at] - base)
        cols = slice(p * width, (p + 1) * width)
        x = x_ref[:, cols]
        parts = []
        for q in range(2):
            done = []
            for i in range(TILES):
                at = slice(i * TILE, (i + 1) * TILE)
                cf, cr = [
                    jnp.broadcast_to(col_ref[p, r : r + 1, at], (TILE, TILE)).T for r in (q, 2 + q)
                ]
                pieces = []
                for j in range(TILES):
                    to = slice(j * TILE, (j + 1) * TILE)
                    rf = row_ref[p, i, q : q + 1, to]
                    rr = row_ref[p, i, 2 + q : 3 + q, to]
                    score = score_ref[at, to]
                    if j < i:
                        weight = (score * rf) * cf
                    elif j > i:
                        weight = (score * rr) * cr
                    else:
                        weight = score * jnp.where(lower, rf * cf, rr * cr)
                    pieces.append(weight.astype(BF16))
                line = jnp.concatenate(pieces, axis=1)
                if i % 2:
                    both = jnp.concatenate([line_before, line], axis=0)
                    done.append(jnp.dot(both, x, preferred_element_type=F32))
                line_before = line
            parts.append(jnp.concatenate(done, axis=0))
        y = jnp.where(first, parts[0], parts[1])
        out_ref[:, cols] = y + skip_ref[:, cols] * x.astype(F32)


def fetch(source, target, sem):
    copy = pltpu.make_async_copy(source, target, sem)
    copy.start()
    return copy


def carried_kernel(headdim, a_hbm, gate_hbm, c_hbm, cum_hbm, before_hbm, off_hbm, in_ref, out_ref, sq_ref, *refs):
    a_buf, gate_buf, c_buf, cum_buf, before_buf, off_buf, hot_ref, sems = refs
    blocks, pairs = a_buf.shape[0], cum_buf.shape[1]
    width = 2 * headdim

    half_lanes = pairs * width // 2

    def copies(k, side):
        at = pl.ds(k * BLOCK, BLOCK)
        if side is None:
            pieces = [
                (off_hbm.at[k], off_buf.at[k]),
                (c_hbm.at[at], c_buf.at[k]),
                (cum_hbm.at[:, :, at], cum_buf.at[k]),
            ]
            sem = 0
        else:
            cols = pl.ds(side * half_lanes, half_lanes)
            pieces = [
                (before_hbm.at[k, :, :, cols], before_buf.at[k, :, :, cols]),
                (gate_hbm.at[at, cols], gate_buf.at[k, :, cols]),
                (a_hbm.at[at, cols], a_buf.at[k, :, cols]),
            ]
            sem = 3 + 3 * side
        return [pltpu.make_async_copy(f, t, sems.at[sem + n, k]) for n, (f, t) in enumerate(pieces)]

    for k in range(blocks):
        for side in (None, 0, 1):
            for copy in copies(k, side):
                copy.start()
    row = lax.broadcasted_iota(jnp.int32, (16 * pairs, 1), 0)
    row = jnp.where(row < 8 * pairs, row, row - 8 * pairs)
    lane = lax.broadcasted_iota(jnp.int32, (1, width), 1)
    for p in range(pairs):
        hot = jnp.where(row == 8 * p + 2 + jnp.where(lane < headdim, 0, 1), 1.0, 0.0)
        hot_ref[:, p * width : (p + 1) * width] = hot.astype(BF16)

    for k in range(blocks):
        for copy in copies(k, None):
            copy.wait()
        every = jnp.exp2(cum_buf[k].reshape(8 * pairs, BLOCK))
        high = every.astype(BF16).astype(F32)
        every_t = jnp.concatenate([high, every - high], axis=0).T.astype(BF16)
        c = c_buf[k]
        cc = jnp.concatenate([c, c], axis=1)
        squares = [jnp.zeros((TILE, width), F32)] * TILES
        scales = [None, None]
        for p in range(pairs):
            if 2 * p % pairs == 0:
                for copy in copies(k, 2 * p // pairs):
                    copy.wait()
            cols = slice(p * width, (p + 1) * width)
            decay = every[8 * p : 8 * p + 8]
            held = [
                halves(before_buf[k, d, :, cols] + off_buf[k, d : d + 1, cols] * in_ref[d, :, cols])
                for d in range(2)
            ]
            held = jnp.concatenate(held, axis=1)
            for part in range(2):
                some = slice(part * BLOCK // 2, (part + 1) * BLOCK // 2)
                if p % 2 == 0:
                    scales[part] = jnp.dot(
                        every_t[some],
                        hot_ref[:, p * width : (p + 2) * width],
                        preferred_element_type=F32,
                    )
                z = jnp.dot(cc[some], held, preferred_element_type=F32)
                for j in range(TILES // 2):
                    i = part * TILES // 2 + j
                    at = slice(i * TILE, (i + 1) * TILE)
                    to = slice(j * TILE, (j + 1) * TILE)
                    rows = [jnp.broadcast_to(decay[r : r + 1, at], (headdim, TILE)) for r in range(2)]
                    total = a_buf[k, at, cols] + jnp.concatenate(rows, axis=0).T * z[to, :width]
                    other = scales[part][to, p % 2 * width : (p % 2 + 1) * width]
                    total = total + other * z[to, width:]
                    half = 0.5 * gate_buf[k, at, cols].astype(F32)
                    gated = total * (half + half * jnp.tanh(half))
                    out_ref[pl.ds(k * BLOCK + i * TILE, TILE), cols] = gated
                    squares[i] = squares[i] + gated * gated
        for i in range(TILES):
            sq_ref[k, :, i * TILE : (i + 1) * TILE] = jnp.sum(squares[i].T, axis=0, keepdims=True)


def norm_kernel(gated_ref, sq_ref, gain_hbm, out_hbm, out_buf, gain_buf, sems, gain_sem):
    blocks = out_buf.shape[0]
    gain = fetch(gain_hbm, gain_buf, gain_sem)
    copy = lambda k: pltpu.make_async_copy(
        out_buf.at[k], out_hbm.at[pl.ds(pl.multiple_of(k * BLOCK, BLOCK), BLOCK)], sems.at[k]
    )
    gain.wait()

    @pl.loop(0, blocks)
    def _(k):
        factor = lax.rsqrt(sq_ref[k] * (1.0 / INNER) + 1e-05)
        factor = jnp.broadcast_to(factor, (128, factor.shape[1])).T
        rows = pl.ds(pl.multiple_of(k * BLOCK, BLOCK), BLOCK)
        for n in range(gated_ref.shape[1] // 128):
            cols = slice(n * 128, (n + 1) * 128)
            out_buf[k, :, cols] = (gated_ref[rows, cols] * factor * gain_buf[:, cols]).astype(BF16)
        copy(k).start()

    @pl.loop(0, blocks)
    def _(k):
        copy(k).wait()


def incoming(finals, beside):
    count, mine = lax.axis_size("seq"), lax.axis_index("seq")
    rows, row, side = count // 2, mine // 2, mine % 2
    left, early = side == 0, row < rows // 2
    swap = [(i, i ^ 1) for i in range(count)]
    send = lambda value, route: lax.ppermute(value, "seq", route)
    groups = range(len(finals))
    stages = [[] for _ in groups]
    state, half = finals[0].shape[1] - 8, finals[0].shape[2] // 2
    kept, given, got1, got2 = {}, {}, {}, {}
    for g in groups:
        first, second = finals[g][:, :, :half], finals[g][:, :, half:]
        kept[g] = jnp.where(left, first, second)
        other = jnp.where(left, second, first)
        given[g] = jnp.where(early, other[0], other[1]), jnp.where(early, other[1], other[0])
        stages[g].append(given[g][0])
        got1[g] = send(given[g][0], swap)
    enter = {g: [jnp.zeros((state, half), F32)] * 2 for g in groups}
    low, high, dl, dh = {}, {}, {}, {}
    got, out1, out2 = {}, {}, {}

    def parts(g, d, arrived):
        mine_d = kept[g][d]
        lo, hi = jnp.where(left, mine_d, arrived), jnp.where(left, arrived, mine_d)
        return lo[:state], hi[:state], lo[state : state + 1], hi[state : state + 1]

    def pair(g, d, pieces):
        lo, hi, decay_lo, decay_hi = pieces
        if d == 0:
            return decay_hi * lo + hi, decay_lo * decay_hi
        return decay_lo * hi + lo, decay_lo * decay_hi

    def both(d, pieces, held):
        lo, hi, decay_lo, decay_hi = pieces
        if d == 0:
            return held, decay_lo * held + lo
        return decay_hi * held + hi, held

    def pick(flag, a, b):
        return jax.tree.map(lambda u, v: jnp.where(flag, u, v), a, b)

    token = early_token = beside(stages[0][-1])
    known = {}
    for hop in range(rows - 1):
        back = rows - 1 - hop
        route = [(2 * hop + s, 2 * hop + 2 + s) for s in range(2)]
        route += [(2 * back + s, 2 * back - 2 + s) for s in range(2)]
        for g in groups:
            if hop == 0:
                known[g] = [parts(g, d, got1[g]) for d in range(2)]
            if hop == rows // 2:
                second = [parts(g, d, got2[g] + token) for d in range(2)]
                known[g] = [pick(early, known[g][0], second[0]), pick(early, second[1], known[g][1])]
            (pf, df), (pr, dr) = pair(g, 0, known[g][0]), pair(g, 1, known[g][1])
            payload = jnp.where(row == hop, df * enter[g][0] + pf, dr * enter[g][1] + pr)
            payload = payload + token
            stages[g].append(payload)
            got[g] = send(payload, route)
        token = beside(stages[0][-1])
        for g in groups:
            if hop == 0:
                later = given[g][1] + (0.0 * got1[g] + early_token)
                got2[g] = send(later, swap)
            enter[g] = [
                jnp.where(row == hop + 1, got[g], enter[g][0]),
                jnp.where(row == back - 1, got[g], enter[g][1]),
            ]
            if hop == max(rows // 2 - 2, 0):
                ends = pick(early, both(0, known[g][0], enter[g][0]), both(1, known[g][1], enter[g][1]))
                out1[g] = (jnp.where(left, ends[0], ends[1]), send(jnp.where(left, ends[1], ends[0]), swap))
    result = []
    for g in groups:
        ends = pick(early, both(1, known[g][1], enter[g][1]), both(0, known[g][0], enter[g][0]))
        payload = jnp.where(left, ends[1], ends[0]) + token
        stages[g].append(payload)
        out2[g] = (jnp.where(left, ends[0], ends[1]), send(payload, swap))
    beside(stages[0][-1])
    for g in groups:
        whole = []
        for own, came in (out1[g], out2[g]):
            whole.append(
                jnp.concatenate([jnp.where(left, own, came), jnp.where(left, came, own)], axis=1)
            )
        result.append(
            jnp.stack([jnp.where(early, whole[0], whole[1]), jnp.where(early, whole[1], whole[0])])
        )
    return result


def shards(activations, gate_input, bmat, cmat, log_fwd, log_rev, skip, gain):
    length, channels = activations.shape
    heads = log_fwd.shape[0]
    headdim = channels // heads
    width = 2 * headdim
    state = bmat.shape[1]
    blocks = length // BLOCK
    pairs = heads // 2
    mine = pairs // GROUPS
    part = channels // GROUPS
    many = 2
    finals = []
    shared = []
    for g in range(GROUPS):
        done = list(shared)
        *shared, final = pl.pallas_call(
            functools.partial(states_kernel, headdim, bool(done)),
            grid=(mine // many,),
            in_specs=[
                pl.BlockSpec((length, many * width), lambda n, g=g: (0, g * mine // many + n)),
                pl.BlockSpec((length, state), lambda n: (0, 0)),
                pl.BlockSpec((2 * mine, length), lambda n, g=g: (g, 0)),
                pl.BlockSpec((2 * mine, length), lambda n, g=g: (g, 0)),
            ]
            + [ANY] * len(done),
            out_specs=[
                pl.BlockSpec((many, 8, length), lambda n, g=g: (g * mine // many + n, 0, 0)),
                pl.BlockSpec(
                    (blocks, 2, state, many * width),
                    lambda n, g=g: (0, 0, 0, g * mine // many + n),
                ),
                pl.BlockSpec((blocks, 8, many * width), lambda n, g=g: (0, 0, g * mine // many + n)),
                pl.BlockSpec((2, state + 8, many * width), lambda n: (0, 0, n)),
            ],
            out_shape=[
                pltpu.HBM((pairs, 8, length), F32),
                pltpu.HBM((blocks, 2, state, channels), F32),
                pltpu.HBM((blocks, 8, channels), F32),
                shape(2, state + 8, part),
            ],
            scratch_shapes=[
                pltpu.VMEM((blocks, state, BLOCK), F32),
                pltpu.VMEM((mine, blocks, 8, BLOCK), F32),
            ],
            input_output_aliases={4 + i: i for i in range(len(done))},
            compiler_params=params(24),
            name="states",
        )(*far(activations, bmat, log_fwd, log_rev, *done))
        finals.append(final)
    cum, before, off = shared
    skip_row = jnp.repeat(skip, headdim)[None]
    within = []
    some = 4
    chunks = pairs // some
    units = blocks * chunks
    cuts = [0] + [units * share // SHARES[-1] for share in SHARES]
    plan = list(zip(cuts[:-1], cuts[1:]))[::-1]

    def piece(dep):
        if not plan:
            return jnp.zeros((1, part // 2), F32)
        start, stop = plan.pop()
        block, chunk = lambda n: (start + n) // chunks, lambda n: lax.rem(start + n, chunks)
        done = list(within)
        within[:1], zero = (lambda out: ([out[0]], out[1]))(
            pl.pallas_call(
                functools.partial(within_kernel, headdim, chunks, start, bool(done)),
                grid=(stop - start,),
                in_specs=[
                    pl.BlockSpec((BLOCK, some * width), lambda n: (block(n), chunk(n))),
                    pl.BlockSpec((BLOCK, state), lambda n: (block(n), 0)),
                    pl.BlockSpec((BLOCK, state), lambda n: (block(n), 0)),
                    pl.BlockSpec((some, 8, BLOCK), lambda n: (chunk(n), 0, block(n))),
                    pl.BlockSpec((1, some * width), lambda n: (0, chunk(n))),
                    ANY,
                ]
                + [ANY] * len(done),
                out_specs=[
                    pl.BlockSpec((BLOCK, some * width), lambda n: (block(n), chunk(n))),
                    pl.BlockSpec((8, part // 2), lambda n: (0, 0)),
                ],
                out_shape=[pltpu.HBM((length, channels), F32), shape(8, part // 2)],
                scratch_shapes=[
                    pltpu.VMEM((BLOCK, BLOCK), F32),
                    pltpu.VMEM((some, TILES, 8, BLOCK), F32),
                    pltpu.VMEM((some, 8, BLOCK), F32),
                ],
                input_output_aliases={6: 0} if done else {},
                compiler_params=params(16),
                cost_estimate=pl.CostEstimate(
                    flops=2 * heads * BLOCK * BLOCK * 512,
                    bytes_accessed=6 * BLOCK * channels,
                    transcendentals=heads * BLOCK * 8,
                ),
                name="within",
            )(*far(activations, bmat, cmat, cum), skip_row, dep, *far(*done))
        )
        return zero[:1]

    enters = incoming(finals, piece)
    while plan:
        piece(finals[0])
    gated, squares = pl.pallas_call(
        functools.partial(carried_kernel, headdim),
        in_specs=[ANY] * 6 + [WHOLE],
        out_specs=[WHOLE, WHOLE],
        out_shape=[pltpu.VMEM((length, channels), F32), shape(blocks, 1, BLOCK)],
        scratch_shapes=[
            pltpu.VMEM((blocks, BLOCK, channels), F32),
            pltpu.VMEM((blocks, BLOCK, channels), BF16),
            pltpu.VMEM((blocks, BLOCK, state), BF16),
            pltpu.VMEM((blocks, pairs, 8, BLOCK), F32),
            pltpu.VMEM((blocks, 2, state, channels), F32),
            pltpu.VMEM((blocks, 8, channels), F32),
            pltpu.VMEM((16 * pairs, channels), BF16),
            pltpu.SemaphoreType.DMA((9, blocks)),
        ],
        compiler_params=pltpu.CompilerParams(vmem_limit_bytes=40 * 1024 * 1024),
        name="carried",
    )(*far(within[0], gate_input, cmat, cum, before, off), enters[0])
    step, size = 1, lax.axis_size("ch")
    while step < size:
        squares = squares + lax.ppermute(squares, "ch", [(i, i ^ step) for i in range(size)])
        step *= 2
    return pl.pallas_call(
        norm_kernel,
        in_specs=[WHOLE, WHOLE, ANY],
        out_specs=ANY,
        out_shape=shape(length, channels, dtype=BF16),
        scratch_shapes=[
            pltpu.VMEM((blocks, BLOCK, channels), BF16),
            pltpu.VMEM((1, channels), F32),
            pltpu.SemaphoreType.DMA((blocks,)),
            pltpu.SemaphoreType.DMA(()),
        ],
        compiler_params=pltpu.CompilerParams(vmem_limit_bytes=24 * 1024 * 1024),
        name="norm",
    )(*near(gated), squares, *far(gain[None]))


def solution(mesh):
    return jax.shard_map(
        shards,
        mesh=mesh,
        in_specs=(
            P("seq", "ch"),
            P("seq", "ch"),
            P("seq", None),
            P("seq", None),
            P("ch", "seq"),
            P("ch", "seq"),
            P("ch"),
            P("ch"),
        ),
        out_specs=P("seq", "ch"),
        check_vma=False,
    )
```
